512 devices in a mesh: ctx: 32 (over x_lo, z), mp: 16 (over y, x_hi, core).
Axes of the slice: x: 4 (x_hi: 2, x_lo: 2; x = x_hi * 2 + x_lo), y: 4, z: 16, core: 2. Of those that a mesh axis runs over, the one named last changes fastest.
Arguments:
- values: bfloat16 [8192, 4096], P('ctx', 'mp'), may hold values from -6 to 6
- gates: bfloat16 [8192, 4096], P('ctx', 'mp'), may hold values from -6 to 6
- cotangent: bfloat16 [8192, 4096], P('ctx', 'mp'), may hold values from -6 to 6
- filters: bfloat16 [8192, 256], P('ctx', 'mp'), may hold values from -6 to 6
- skip_gain: float32 [4096], P('mp'), may hold values from -4 to 4
Outputs:
- grad_gates: bfloat16 [8192, 4096], P('ctx', 'mp')
- grad_values: bfloat16 [8192, 4096], P('ctx', 'mp')
- grad_filters: bfloat16 [8192, 256], P('ctx', 'mp')
The draws below stay inside these ranges and needn't reach their ends.
All inputs are finite; a program needn't handle non-finite values.
Results may differ from the reference program's by a relative error of at most 0.022.
Values may be sent and summed in bfloat16 or wider, within the bound.
No kernel may reach another device: no remote copies, remote signals or barrier semaphores. Data moves between devices by JAX's collectives and lax.ppermute only.
A program may use at most 64 MiB of HBM per device.

```python
import jax
import jax.numpy as jnp
from jax import lax

GROUPS = 256
L = 8192
C = 4096


def steps_of(stream_key, extent, split, least, largest):
    level, own = 1.0, jax.random.fold_in(stream_key, 6)
    for axis_at, parts in split:
        heights = jnp.exp(jax.random.uniform(jax.random.fold_in(own, axis_at), (parts,), jnp.float32, least / len(split), largest / len(split)))
        level = level * jnp.repeat(heights, extent[axis_at] // parts).reshape([-1 if axis == axis_at else 1 for axis in range(len(extent))])
    return level


def centred(stream_key, dims, spread, most, pieces=(), dtype=jnp.bfloat16):
    gain = steps_of(stream_key, dims, pieces, -0.22, 0.18) if pieces else 1.0
    result = jax.random.normal(stream_key, dims, jnp.float32) * spread * gain
    return jnp.minimum(jnp.maximum(result, -most), most).astype(dtype)


def setup_inputs(seed: int = 0) -> dict:
    keys = jax.random.split(jax.random.key(seed), 6)
    values = centred(keys[0], (L, C), 1.0, 6.0, ((0, 32), (1, 16)))
    gates = centred(keys[1], (L, C), 1.0, 6.0, ((0, 32), (1, 16)))
    cotangent = centred(keys[2], (L, C), 1.0, 6.0, ((0, 32), (1, 16)))
    filters = centred(keys[3], (L, GROUPS), 1.0, 6.0, ((0, 32), (1, 16)))
    skip_gain = centred(keys[4], (C,), 1.0, 4.0, ((0, 16),), jnp.float32)
    return dict(values=values, gates=gates, cotangent=cotangent, filters=filters, skip_gain=skip_gain)


def reference(values, gates, cotangent, filters, skip_gain):
    repeats = C // GROUPS
    points = 2 * L
    factor = 1.0 / (L ** 0.5)
    gated = (cotangent.astype(jnp.float32) * gates.astype(jnp.float32)).astype(jnp.bfloat16)
    filter_spec = jnp.fft.rfft(filters.astype(jnp.float32), n=points, axis=0) * factor

    def split_blocks(array):
        return jnp.transpose(array.reshape(L, repeats, GROUPS), (1, 0, 2))

    def one_block(summed, inputs):
        value_blk, cot_blk, gated_blk, skip_blk = inputs
        value_f = value_blk.astype(jnp.float32)
        gated_f = gated_blk.astype(jnp.float32)
        value_spec = jnp.fft.rfft(value_f, n=points, axis=0)
        gated_spec = jnp.fft.rfft(gated_f, n=points, axis=0)
        conv = jnp.fft.irfft(filter_spec * value_spec, n=points, axis=0)[:L]
        back = jnp.fft.irfft(jnp.conj(filter_spec) * gated_spec, n=points, axis=0)[:L]
        lagged = jnp.fft.irfft(gated_spec * jnp.conj(value_spec), n=points, axis=0)[:L]
        grad_gate = (cot_blk.astype(jnp.float32) * (conv + skip_blk[None, :] * value_f)).astype(jnp.bfloat16)
        grad_value = (back + skip_blk[None, :] * gated_f).astype(jnp.bfloat16)
        return summed + lagged, (grad_gate, grad_value)

    inputs = (split_blocks(values), split_blocks(cotangent), split_blocks(gated),
              skip_gain.reshape(repeats, GROUPS))
    summed, outputs = lax.scan(one_block, jnp.zeros((L, GROUPS), jnp.float32), inputs)
    grad_gates = jnp.transpose(outputs[0], (1, 0, 2)).reshape(L, C)
    grad_values = jnp.transpose(outputs[1], (1, 0, 2)).reshape(L, C)
    grad_filters = (summed * factor).astype(jnp.bfloat16)
    return grad_gates, grad_values, grad_filters
```

```python
import functools
import math

import jax
import jax.numpy as jnp
import numpy as np
from jax import lax
from jax.experimental import pallas as pl
from jax.experimental.pallas import tpu as pltpu
from jax.sharding import PartitionSpec as P

BLOCKS = 32
HALF = 16
MINE = 8
WIDTH = 256
LENGTH = BLOCKS * WIDTH
SHARDS = 16
FACTOR = 1.0 / math.sqrt(LENGTH)
VMEM = 32 * 1024 * 1024


def tables():
    quarter = np.arange(BLOCKS) + 0.25
    outer = 2.0 * np.pi * np.outer(quarter, np.arange(BLOCKS)) / BLOCKS
    eye = np.eye(MINE)
    cos_rows = np.kron(np.cos(outer), eye)
    sin_rows = np.kron(np.sin(outer), eye)
    first = np.concatenate([cos_rows, -sin_rows], 0)
    last = np.concatenate([cos_rows.T, sin_rows.T], 1)
    by_channel = np.arange(BLOCKS * MINE).reshape(BLOCKS, MINE).T.reshape(-1)
    inner = 2.0 * np.pi * (np.outer(np.arange(WIDTH), np.arange(WIDTH)) % WIDTH) / WIDTH
    cos_in, sin_in = (np.cos(inner), np.sin(inner))
    middle = np.block([[cos_in, -sin_in], [sin_in, cos_in]])
    twist = 2.0 * np.pi * np.outer(quarter, np.arange(WIDTH)) / LENGTH
    twist = np.repeat(twist, MINE, axis=0)
    packed = np.arange(WIDTH).reshape(2, MINE, HALF).transpose(0, 2, 1).reshape(-1)
    order = np.zeros((WIDTH, WIDTH))
    order[np.arange(WIDTH), packed] = 1.0
    twice = np.concatenate([np.eye(HALF), np.eye(HALF)], 0)
    low = lambda array: array.astype(np.float32).astype(jnp.bfloat16)
    return dict(
        first=low(first),
        first_by_channel=low(first[:, by_channel]),
        middle=low(middle),
        last=low(last),
        last_by_channel=low(last[by_channel]),
        twist_cos=np.cos(twist).astype(np.float32),
        twist_sin=np.sin(twist).astype(np.float32),
        order=low(order),
        twice=low(twice),
        eye=low(np.eye(HALF)),
    )


def dot(left, right, dims=((1,), (0,))):
    return lax.dot_general(
        left.astype(jnp.bfloat16),
        right.astype(jnp.bfloat16),
        (dims, ((), ())),
        preferred_element_type=jnp.float32,
    )


def twisted(real, imag, cos, sin):
    return jnp.concatenate([real * cos + imag * sin, imag * cos - real * sin], 1)


def forward(rows, first, middle, cos, sin):
    both = dot(first, rows)
    half = both.shape[0] // 2
    return dot(twisted(both[:half], both[half:], cos, sin), middle)


def inverse(real, imag, middle, last, cos, sin):
    both = dot(jnp.concatenate([real, imag], 1), middle)
    both = twisted(both[:, :WIDTH], both[:, WIDTH:], cos, sin)
    both = jnp.concatenate([both[:, :WIDTH], both[:, WIDTH:]], 0)
    return dot(last, both)


def parts_of(spectrum):
    return (spectrum[:, :WIDTH], spectrum[:, WIDTH:])


def pack(upper, lower, extra):
    pieces = []
    for rows in (upper, lower):
        rows = rows.reshape(BLOCKS, MINE, WIDTH)
        pieces += [rows[:, :, :128], rows[:, :, 128:]]
    shape = (BLOCKS, MINE // 2, 128)
    for piece in (extra[:, :128], extra[:, 128:]):
        pieces.append(jnp.broadcast_to(piece[:, None, :], shape))
    return jnp.concatenate(pieces, 1).astype(jnp.bfloat16)


def rows_of(block, at):
    block = block.astype(jnp.float32)
    left = block[:, at : at + MINE].reshape(BLOCKS * MINE, 128)
    right = block[:, at + MINE : at + 2 * MINE].reshape(BLOCKS * MINE, 128)
    return jnp.concatenate([left, right], 1)


def extra_of(block):
    block = block[:, 4 * MINE :].astype(jnp.float32)
    return jnp.concatenate([block[:, 0], block[:, MINE // 2]], 1)


def product_of(cotangent, gates):
    return (cotangent.astype(jnp.float32) * gates.astype(jnp.float32)).astype(jnp.bfloat16)


def outgoing(values, gates, cotangent, filters, order, twice):
    gated = product_of(cotangent, gates)
    across = ((1,), (1,))
    return pack(dot(order, values, across), dot(order, gated, across), dot(twice, filters, across))


def spectra(block, first, middle, last_by_channel, cos, sin):
    value = forward(rows_of(block, 0), first, middle, cos, sin)
    gated = forward(rows_of(block, 2 * MINE), first, middle, cos, sin)
    (value_r, value_i), (gated_r, gated_i) = (parts_of(value), parts_of(gated))
    lagged = inverse(
        gated_r * value_r + gated_i * value_i,
        gated_r * value_i - gated_i * value_r,
        middle, last_by_channel, cos, sin,
    ) * (1.0 / LENGTH)
    lagged = lagged.reshape(MINE, BLOCKS, WIDTH)
    own = jnp.broadcast_to(extra_of(block)[None], (SHARDS, BLOCKS, WIDTH))
    sent = jnp.concatenate([jnp.concatenate([lagged, lagged], 0), own], 1).astype(jnp.bfloat16)
    return (value, gated, sent)


def results(filters, lagged, value, gated, first_by_channel, middle, last, cos, sin):
    filt = forward(filters.reshape(MINE * BLOCKS, WIDTH), first_by_channel, middle, cos, sin)
    (filt_r, filt_i) = parts_of(filt)
    (value_r, value_i), (gated_r, gated_i) = (parts_of(value), parts_of(gated))
    scale = FACTOR / LENGTH
    conv = inverse(
        filt_r * value_r - filt_i * value_i,
        -filt_r * value_i - filt_i * value_r,
        middle, last, cos, sin,
    ) * scale
    back = inverse(
        filt_r * gated_r + filt_i * gated_i,
        filt_i * gated_r - filt_r * gated_i,
        middle, last, cos, sin,
    ) * scale
    total = lagged.astype(jnp.float32).sum(0) * FACTOR
    return pack(conv, back, total)


def finished(block, mine, values, gates, cotangent, skip_row, order, eye):
    down = ((0,), (0,))
    conv = dot(rows_of(block, 0), order, down)
    back = dot(rows_of(block, 2 * MINE), order, down)
    gated = product_of(cotangent, gates).astype(jnp.float32)
    grad_gates = cotangent.astype(jnp.float32) * (conv + skip_row * values.astype(jnp.float32))
    grad_values = back + skip_row * gated
    grad_filters = dot(extra_of(mine), eye, down)
    return tuple(out.astype(jnp.bfloat16) for out in (grad_gates, grad_values, grad_filters))


def outgoing_kernel(*refs):
    refs[-1][...] = outgoing(*(ref[...] for ref in refs[:-1]))


def spectra_kernel(*refs):
    outs = spectra(*(ref[...] for ref in refs[:-3]))
    for ref, out in zip(refs[-3:], outs):
        ref[...] = out


def results_kernel(place, arrived, *refs):
    start = pl.multiple_of(place[0] * MINE, MINE)
    filters = arrived[pl.ds(start, MINE), BLOCKS:, :]
    lagged = arrived[:, :BLOCKS, :]
    refs[-1][...] = results(filters, lagged, *(ref[...] for ref in refs[:-1]))


def finished_kernel(place, block, *refs):
    start = pl.multiple_of(place[0] * HALF, HALF)
    mine = block[pl.ds(start, HALF)]
    outs = finished(block[...], mine, *(ref[...] for ref in refs[:-3]))
    for ref, out in zip(refs[-3:], outs):
        ref[...] = out


def call(kernel, outs, args, flops, scalars=0):
    whole = pl.BlockSpec(memory_space=pltpu.VMEM)
    scalar = pl.BlockSpec(memory_space=pltpu.SMEM)
    size = sum(math.prod(out.shape) * out.dtype.itemsize for out in (*outs, *args))
    single = len(outs) == 1
    return pl.pallas_call(
        kernel,
        out_shape=outs[0] if single else outs,
        in_specs=[scalar] * scalars + [whole] * (len(args) - scalars),
        out_specs=whole if single else (whole,) * len(outs),
        compiler_params=pltpu.CompilerParams(vmem_limit_bytes=VMEM),
        cost_estimate=pl.CostEstimate(flops=flops, bytes_accessed=size, transcendentals=0),
    )(*args)


def swap(block, axis):
    return lax.all_to_all(block, axis, split_axis=0, concat_axis=0, tiled=True)


def per_device(table, values, gates, cotangent, filters, skip_gain):
    shape = functools.partial(jax.ShapeDtypeStruct, dtype=jnp.bfloat16)
    spectrum = jax.ShapeDtypeStruct((WIDTH, 2 * WIDTH), jnp.float32)
    packed = shape((BLOCKS, 5 * MINE, 128))
    ctx_half = (lax.axis_index("ctx") // HALF).astype(jnp.int32).reshape(1)
    mp_half = (lax.axis_index("mp") // MINE).astype(jnp.int32).reshape(1)
    twist = (table["twist_cos"], table["twist_sin"])
    cube = 2 * WIDTH**3

    block = call(
        outgoing_kernel, (packed,),
        (values, gates, cotangent, filters, table["order"], table["twice"]), 2 * cube,
    )
    block = swap(block, "ctx")
    value, gated, sent = call(
        spectra_kernel, (spectrum, spectrum, shape((SHARDS, 2 * BLOCKS, WIDTH))),
        (block, table["first"], table["middle"], table["last_by_channel"], *twist), 18 * cube,
    )
    sent = swap(sent, "mp")
    block = call(
        results_kernel, (packed,),
        (ctx_half, sent, value, gated, table["first_by_channel"], table["middle"], table["last"], *twist),
        18 * cube, scalars=1,
    )
    block = swap(block, "ctx")
    return call(
        finished_kernel, (shape(values.shape), shape(values.shape), shape(filters.shape)),
        (mp_half, block, values, gates, cotangent, skip_gain[None, :], table["order"], table["eye"]),
        2 * cube, scalars=1,
    )


def solution(mesh):
    return jax.shard_map(
        functools.partial(per_device, tables()),
        mesh=mesh,
        in_specs=(P("ctx", "mp"), P("ctx", "mp"), P("ctx", "mp"), P("ctx", "mp"), P("mp")),
        out_specs=(P("ctx", "mp"), P("ctx", "mp"), P("ctx", "mp")),
        check_vma=False,
    )
```

```python
import functools
import math

import jax
import jax.numpy as jnp
import numpy as np
from jax import lax
from jax.experimental import pallas as pl
from jax.experimental.pallas import tpu as pltpu
from jax.sharding import PartitionSpec as P

BLOCKS = 32
HALF = 16
MINE = 8
WIDTH = 256
LENGTH = BLOCKS * WIDTH
SHARDS = 16
FACTOR = 1.0 / math.sqrt(LENGTH)
VMEM = 32 * 1024 * 1024


def tables():
    quarter = np.arange(BLOCKS) + 0.25
    outer = 2.0 * np.pi * np.outer(quarter, np.arange(BLOCKS)) / BLOCKS
    eye = np.eye(MINE)
    cos_rows = np.kron(np.cos(outer), eye)
    sin_rows = np.kron(np.sin(outer), eye)
    first = np.concatenate([cos_rows, -sin_rows], 0)
    last = np.concatenate([cos_rows.T, sin_rows.T], 1)
    by_channel = np.arange(BLOCKS * MINE).reshape(BLOCKS, MINE).T.reshape(-1)
    inner = 2.0 * np.pi * (np.outer(np.arange(WIDTH), np.arange(WIDTH)) % WIDTH) / WIDTH
    cos_in, sin_in = (np.cos(inner), np.sin(inner))
    middle = np.block([[cos_in, -sin_in], [sin_in, cos_in]])
    twist = 2.0 * np.pi * np.outer(quarter, np.arange(WIDTH)) / LENGTH
    twist = np.repeat(twist, MINE, axis=0)
    low = lambda array: array.astype(np.float32).astype(jnp.bfloat16)
    return dict(
        first=low(first),
        first_by_channel=low(first[:, by_channel]),
        middle=low(middle),
        last=low(last),
        last_by_channel=low(last[by_channel]),
        twist_cos=np.cos(twist).astype(np.float32),
        twist_sin=np.sin(twist).astype(np.float32),
    )


def dot(left, right, dims=((1,), (0,))):
    return lax.dot_general(
        left.astype(jnp.bfloat16),
        right.astype(jnp.bfloat16),
        (dims, ((), ())),
        preferred_element_type=jnp.float32,
    )


def order_of():
    row = lax.broadcasted_iota(jnp.int32, (WIDTH, WIDTH), 0)
    channel = lax.broadcasted_iota(jnp.int32, (WIDTH, WIDTH), 1)
    wanted = ((row >> 7) << 7) + ((row & 7) << 4) + ((row >> 3) & 15)
    return (channel == wanted).astype(jnp.float32).astype(jnp.bfloat16)


def twisted(real, imag, cos, sin):
    return jnp.concatenate([real * cos + imag * sin, imag * cos - real * sin], 1)


def forward(rows, first, middle, cos, sin):
    both = dot(first, rows)
    half = both.shape[0] // 2
    return dot(twisted(both[:half], both[half:], cos, sin), middle)


def inverse(real, imag, middle, last, cos, sin):
    both = dot(jnp.concatenate([real, imag], 1), middle)
    both = twisted(both[:, :WIDTH], both[:, WIDTH:], cos, sin)
    both = jnp.concatenate([both[:, :WIDTH], both[:, WIDTH:]], 0)
    return dot(last, both)


def parts_of(spectrum):
    return (spectrum[:, :WIDTH], spectrum[:, WIDTH:])


def pack(upper, lower, extra):
    pieces = []
    for rows in (upper, lower):
        rows = rows.reshape(BLOCKS, MINE, WIDTH)
        pieces += [rows[:, :, :128], rows[:, :, 128:]]
    shape = (BLOCKS, MINE // 2, 128)
    for piece in (extra[:, :128], extra[:, 128:]):
        pieces.append(jnp.broadcast_to(piece[:, None, :], shape))
    return jnp.concatenate(pieces, 1).astype(jnp.bfloat16)


def rows_of(block, at):
    block = block.astype(jnp.float32)
    left = block[:, at : at + MINE].reshape(BLOCKS * MINE, 128)
    right = block[:, at + MINE : at + 2 * MINE].reshape(BLOCKS * MINE, 128)
    return jnp.concatenate([left, right], 1)


def extra_of(block):
    block = block[:, 4 * MINE :].astype(jnp.float32)
    return jnp.concatenate([block[:, 0], block[:, MINE // 2]], 1)


def product_of(cotangent, gates):
    return (cotangent.astype(jnp.float32) * gates.astype(jnp.float32)).astype(jnp.bfloat16)


def outgoing(values, gates, cotangent, filters):
    gated = product_of(cotangent, gates)
    across = ((1,), (1,))
    order = order_of()
    twice = jnp.concatenate([filters, filters], 0).astype(jnp.float32)
    return pack(dot(order, values, across), dot(order, gated, across), twice)


def spectra(block, first, middle, last_by_channel, cos, sin):
    value = forward(rows_of(block, 0), first, middle, cos, sin)
    gated = forward(rows_of(block, 2 * MINE), first, middle, cos, sin)
    (value_r, value_i), (gated_r, gated_i) = (parts_of(value), parts_of(gated))
    lagged = inverse(
        gated_r * value_r + gated_i * value_i,
        gated_r * value_i - gated_i * value_r,
        middle, last_by_channel, cos, sin,
    ) * (1.0 / LENGTH)
    lagged = lagged.reshape(MINE, BLOCKS, WIDTH)
    own = jnp.broadcast_to(extra_of(block)[None], (SHARDS, BLOCKS, WIDTH))
    sent = jnp.concatenate([jnp.concatenate([lagged, lagged], 0), own], 1).astype(jnp.bfloat16)
    return (value, gated, sent)


def results(filters, lagged, value, gated, first_by_channel, middle, last, cos, sin):
    filt = forward(filters.reshape(MINE * BLOCKS, WIDTH), first_by_channel, middle, cos, sin)
    (filt_r, filt_i) = parts_of(filt)
    (value_r, value_i), (gated_r, gated_i) = (parts_of(value), parts_of(gated))
    scale = FACTOR / LENGTH
    conv = inverse(
        filt_r * value_r - filt_i * value_i,
        -filt_r * value_i - filt_i * value_r,
        middle, last, cos, sin,
    ) * scale
    back = inverse(
        filt_r * gated_r + filt_i * gated_i,
        filt_i * gated_r - filt_r * gated_i,
        middle, last, cos, sin,
    ) * scale
    total = lagged.astype(jnp.float32).sum(0) * FACTOR
    return pack(conv, back, total)


def finished(block, mine, values, gates, cotangent, skip_row):
    down = ((0,), (0,))
    order = order_of()
    conv = dot(rows_of(block, 0), order, down)
    back = dot(rows_of(block, 2 * MINE), order, down)
    gated = product_of(cotangent, gates).astype(jnp.float32)
    grad_gates = cotangent.astype(jnp.float32) * (conv + skip_row * values.astype(jnp.float32))
    grad_values = back + skip_row * gated
    grad_filters = extra_of(mine)
    return tuple(out.astype(jnp.bfloat16) for out in (grad_gates, grad_values, grad_filters))


def outgoing_kernel(values, gates, cotangent, filters, skip, out, skip_out, *scratch):
    held, sems = (scratch[:-1], scratch[-1])
    copies = []
    for at, (source, target) in enumerate(zip((values, gates, cotangent, filters, skip), held)):
        copies.append(pltpu.make_async_copy(source, target, sems.at[at]))
        copies[-1].start()
    for copy in copies:
        copy.wait()
    out[...] = outgoing(*(ref[...] for ref in held[:-1]))
    skip_out[...] = held[-1][...]


def spectra_kernel(*refs):
    outs = spectra(*(ref[...] for ref in refs[:-3]))
    for ref, out in zip(refs[-3:], outs):
        ref[...] = out


def results_kernel(place, arrived, *refs):
    start = pl.multiple_of(place[0] * MINE, MINE)
    filters = arrived[pl.ds(start, MINE), BLOCKS:, :]
    lagged = arrived[:, :BLOCKS, :]
    refs[-1][...] = results(filters, lagged, *(ref[...] for ref in refs[:-1]))


def finished_kernel(place, block, *refs):
    start = pl.multiple_of(place[0] * HALF, HALF)
    mine = block[pl.ds(start, HALF)]
    outs = finished(block[...], mine, *(ref[...] for ref in refs[:-3]))
    for ref, out in zip(refs[-3:], outs):
        ref[...] = out


def call(kernel, outs, args, flops, scalars=0, fetched=False):
    whole = pl.BlockSpec(memory_space=pltpu.VMEM)
    scalar = pl.BlockSpec(memory_space=pltpu.SMEM)
    given = pl.BlockSpec(memory_space=pl.ANY) if fetched else whole
    size = sum(math.prod(out.shape) * out.dtype.itemsize for out in (*outs, *args))
    single = len(outs) == 1
    scratch = []
    if fetched:
        scratch = [pltpu.VMEM(arg.shape, arg.dtype) for arg in args]
        scratch.append(pltpu.SemaphoreType.DMA((len(args),)))
    return pl.pallas_call(
        kernel,
        out_shape=outs[0] if single else outs,
        in_specs=[scalar] * scalars + [given] * (len(args) - scalars),
        out_specs=whole if single else (whole,) * len(outs),
        scratch_shapes=scratch,
        compiler_params=pltpu.CompilerParams(vmem_limit_bytes=VMEM),
        cost_estimate=pl.CostEstimate(flops=flops, bytes_accessed=size, transcendentals=0),
    )(*args)


def swap(block, axis):
    return lax.all_to_all(block, axis, split_axis=0, concat_axis=0, tiled=True)


def per_device(table, values, gates, cotangent, filters, skip_gain):
    shape = functools.partial(jax.ShapeDtypeStruct, dtype=jnp.bfloat16)
    spectrum = jax.ShapeDtypeStruct((WIDTH, 2 * WIDTH), jnp.float32)
    packed = shape((BLOCKS, 5 * MINE, 128))
    ctx_half = (lax.axis_index("ctx") // HALF).astype(jnp.int32).reshape(1)
    mp_half = (lax.axis_index("mp") // MINE).astype(jnp.int32).reshape(1)
    twist = (table["twist_cos"], table["twist_sin"])
    cube = 2 * WIDTH**3

    skip_shape = jax.ShapeDtypeStruct((1, WIDTH), jnp.float32)
    block, skip_row = call(
        outgoing_kernel, (packed, skip_shape),
        (values, gates, cotangent, filters.T, skip_gain[None, :]), 2 * cube, fetched=True,
    )
    block = swap(block, "ctx")
    value, gated, sent = call(
        spectra_kernel, (spectrum, spectrum, shape((SHARDS, 2 * BLOCKS, WIDTH))),
        (block, table["first"], table["middle"], table["last_by_channel"], *twist), 18 * cube,
    )
    sent = swap(sent, "mp")
    block = call(
        results_kernel, (packed,),
        (ctx_half, sent, value, gated, table["first_by_channel"], table["middle"], table["last"], *twist),
        18 * cube, scalars=1,
    )
    block = swap(block, "ctx")
    grad_gates, grad_values, grad_filters = call(
        finished_kernel, (shape(values.shape), shape(values.shape), shape((HALF, WIDTH))),
        (mp_half, block, values, gates, cotangent, skip_row), 2 * cube, scalars=1,
    )
    return (grad_gates, grad_values, grad_filters.T)


def solution(mesh):
    return jax.shard_map(
        functools.partial(per_device, tables()),
        mesh=mesh,
        in_specs=(P("ctx", "mp"), P("ctx", "mp"), P("ctx", "mp"), P("ctx", "mp"), P("mp")),
        out_specs=(P("ctx", "mp"), P("ctx", "mp"), P("ctx", "mp")),
        check_vma=False,
    )
```

```python
import functools
import math

import jax
import jax.numpy as jnp
import numpy as np
from jax import lax
from jax.experimental import pallas as pl
from jax.experimental.pallas import tpu as pltpu
from jax.sharding import PartitionSpec as P

BLOCKS = 32
HALF = 16
MINE = 8
WIDTH = 256
LENGTH = BLOCKS * WIDTH
SHARDS = 16
FACTOR = 1.0 / math.sqrt(LENGTH)
VMEM = 32 * 1024 * 1024
MOST = 63 * 1024 * 1024


def tables():
    quarter = np.arange(BLOCKS) + 0.25
    outer = 2.0 * np.pi * np.outer(quarter, np.arange(BLOCKS)) / BLOCKS
    eye = np.eye(MINE)
    cos_rows = np.kron(np.cos(outer), eye)
    sin_rows = np.kron(np.sin(outer), eye)
    first = np.concatenate([cos_rows, -sin_rows], 0)
    last = np.concatenate([cos_rows.T, sin_rows.T], 1)
    by_channel = np.arange(BLOCKS * MINE).reshape(BLOCKS, MINE).T.reshape(-1)
    inner = 2.0 * np.pi * (np.outer(np.arange(WIDTH), np.arange(WIDTH)) % WIDTH) / WIDTH
    cos_in, sin_in = (np.cos(inner), np.sin(inner))
    twist = 2.0 * np.pi * np.outer(quarter, np.arange(WIDTH)) / LENGTH
    low = lambda array: array.astype(np.float32).astype(jnp.bfloat16)
    return dict(
        first=low(first),
        first_by_channel=low(first[:, by_channel]),
        middle=low(np.concatenate([cos_in, sin_in], 1)),
        last=low(last),
        last_by_channel=low(last[by_channel]),
        twist=np.stack([np.cos(twist), np.sin(twist)]).astype(np.float32),
    )


def dot(left, right, dims=((1,), (0,))):
    return lax.dot_general(
        left.astype(jnp.bfloat16),
        right.astype(jnp.bfloat16),
        (dims, ((), ())),
        preferred_element_type=jnp.float32,
    )


def source_of(half, row, place):
    return jnp.where(row == 0, 8 * half + (place & 7), (place - row - 8 * half) & 15)


def order_of(place):
    row = lax.broadcasted_iota(jnp.int32, (WIDTH, WIDTH), 0)
    channel = lax.broadcasted_iota(jnp.int32, (WIDTH, WIDTH), 1)
    wanted = 16 * source_of(row >> 7, row & 7, place) + ((row >> 3) & 15)
    return (channel == wanted).astype(jnp.float32).astype(jnp.bfloat16)


def whirl(both, middle, twist_first, twist):
    if twist_first:
        both = twisted(both, twist)
    terms = dot(both, middle)
    real, imag = (terms[:WIDTH], terms[WIDTH:])
    both = jnp.concatenate(
        [real[:, :WIDTH] + imag[:, WIDTH:], imag[:, :WIDTH] - real[:, WIDTH:]], 0
    )
    return both if twist_first else twisted(both, twist)


def twisted(both, twist):
    shape = (BLOCKS, MINE, WIDTH)
    cos, sin = (twist[0][:, None, :], twist[1][:, None, :])
    real, imag = (both[:WIDTH].reshape(shape), both[WIDTH:].reshape(shape))
    both = jnp.concatenate([real * cos + imag * sin, imag * cos - real * sin], 0)
    return both.reshape(2 * WIDTH, WIDTH)


def forward(rows, first, middle, twist):
    return whirl(dot(first, rows), middle, True, twist)


def inverse(real, imag, middle, last, twist):
    return dot(last, whirl(jnp.concatenate([real, imag], 0), middle, False, twist))


def parts_of(spectrum):
    return (spectrum[:WIDTH], spectrum[WIDTH:])


def pack(upper, lower, extra):
    pieces = []
    for rows in (upper, lower):
        rows = rows.reshape(BLOCKS, MINE, WIDTH)
        pieces += [rows[:, :, :128], rows[:, :, 128:]]
    shape = (BLOCKS, MINE // 2, 128)
    for piece in (extra[:, :128], extra[:, 128:]):
        pieces.append(jnp.broadcast_to(piece[:, None, :], shape))
    return jnp.concatenate(pieces, 1).astype(jnp.bfloat16)


def rows_of(block, at):
    block = block.astype(jnp.float32)
    left = block[:, at : at + MINE].reshape(BLOCKS * MINE, 128)
    right = block[:, at + MINE : at + 2 * MINE].reshape(BLOCKS * MINE, 128)
    return jnp.concatenate([left, right], 1)


def extra_of(block):
    block = block[:, 4 * MINE :].astype(jnp.float32)
    return jnp.concatenate([block[:, 0], block[:, MINE // 2]], 1)


def product_of(cotangent, gates):
    return (cotangent.astype(jnp.float32) * gates.astype(jnp.float32)).astype(jnp.bfloat16)


def outgoing(place, values, gates, cotangent, filters):
    gated = product_of(cotangent, gates)
    across = ((1,), (1,))
    order = order_of(place)
    twice = jnp.concatenate([filters, filters], 0).astype(jnp.float32)
    return pack(dot(order, values, across), dot(order, gated, across), twice)


def spectra(block, first, middle, last_by_channel, twist):
    value = forward(rows_of(block, 0), first, middle, twist)
    gated = forward(rows_of(block, 2 * MINE), first, middle, twist)
    (value_r, value_i), (gated_r, gated_i) = (parts_of(value), parts_of(gated))
    lagged = inverse(
        gated_r * value_r + gated_i * value_i,
        gated_r * value_i - gated_i * value_r,
        middle, last_by_channel, twist,
    ) * (1.0 / LENGTH)
    lagged = lagged.reshape(MINE, BLOCKS, WIDTH)
    return (value, gated, lagged.astype(jnp.bfloat16), extra_of(block).astype(jnp.bfloat16))


def results(filters, total, value, gated, first_by_channel, middle, last, twist):
    filt = forward(filters.reshape(MINE * BLOCKS, WIDTH), first_by_channel, middle, twist)
    (filt_r, filt_i) = parts_of(filt)
    (value_r, value_i), (gated_r, gated_i) = (parts_of(value), parts_of(gated))
    scale = FACTOR / LENGTH
    conv = inverse(
        filt_r * value_r - filt_i * value_i,
        -filt_r * value_i - filt_i * value_r,
        middle, last, twist,
    ) * scale
    back = inverse(
        filt_r * gated_r + filt_i * gated_i,
        filt_i * gated_r - filt_r * gated_i,
        middle, last, twist,
    ) * scale
    return pack(conv, back, total * FACTOR)


def finished(place, block, values, gates, cotangent, skip_rows):
    down = ((0,), (0,))
    order = order_of(place)
    conv = dot(rows_of(block, 0), order, down)
    back = dot(rows_of(block, 2 * MINE), order, down)
    gated = product_of(cotangent, gates).astype(jnp.float32)
    grad_gates = cotangent.astype(jnp.float32) * (conv + skip_rows[:1] * values.astype(jnp.float32))
    grad_values = back + skip_rows[:1] * gated
    partial = extra_of(block)
    grad_filters = partial[:HALF] + partial[HALF:]
    return tuple(out.astype(jnp.bfloat16) for out in (grad_gates, grad_values, grad_filters))


def outgoing_kernel(mp_place, values, gates, cotangent, filters, out, *scratch):
    held, sems = (scratch[:-1], scratch[-1])
    copies = []
    for at, (source, target) in enumerate(zip((values, gates, cotangent, filters), held)):
        copies.append(pltpu.make_async_copy(source, target, sems.at[at]))
        copies[-1].start()
    for copy in copies:
        copy.wait()
    out[...] = outgoing(mp_place[0], *(ref[...] for ref in held))


def spectra_kernel(ctx_half, mp_place, *refs):
    half, place = (ctx_half[0], mp_place[0])
    value, gated, own, sent = refs[-4:]
    value[...], gated[...], lagged, own_rows = spectra(*(ref[...] for ref in refs[:-4]))
    own[...] = own_rows
    sent[...] = jnp.broadcast_to(own_rows[None], sent.shape)
    for row in range(MINE):
        sent[source_of(half, row, place)] = lagged[row]


def results_kernel(ctx_half, mp_place, arrived, own, *refs):
    half, place = (ctx_half[0], mp_place[0])
    held = source_of(half, 0, place) == place
    filters = [jnp.where(held, own[...], arrived[source_of(half, 0, place)])]
    filters += [arrived[source_of(half, row, place)] for row in range(1, MINE)]
    total = jnp.zeros((BLOCKS, WIDTH), jnp.float32)
    for other in range(SHARDS):
        ahead = (other - place) & 15
        near = (ahead >= 1) & (ahead <= 7) | (place == other & 7)
        total += jnp.where(near == (half == 0), arrived[other].astype(jnp.float32), 0.0)
    refs[-1][...] = results(jnp.stack(filters), total, *(ref[...] for ref in refs[:-1]))


def finished_kernel(mp_place, *refs):
    outs = finished(mp_place[0], *(ref[...] for ref in refs[:-3]))
    for ref, out in zip(refs[-3:], outs):
        ref[...] = out


def call(kernel, outs, args, flops, scalars=0, fetched=False):
    whole = pl.BlockSpec(memory_space=pltpu.VMEM)
    scalar = pl.BlockSpec(memory_space=pltpu.SMEM)
    given = pl.BlockSpec(memory_space=pl.ANY) if fetched else whole
    size = sum(math.prod(out.shape) * out.dtype.itemsize for out in (*outs, *args))
    single = len(outs) == 1
    scratch = []
    if fetched:
        scratch = [pltpu.VMEM(arg.shape, arg.dtype) for arg in args[scalars:]]
        scratch.append(pltpu.SemaphoreType.DMA((len(scratch),)))
    return pl.pallas_call(
        kernel,
        out_shape=outs[0] if single else outs,
        in_specs=[scalar] * scalars + [given] * (len(args) - scalars),
        out_specs=whole if single else (whole,) * len(outs),
        scratch_shapes=scratch,
        compiler_params=pltpu.CompilerParams(vmem_limit_bytes=MOST if fetched else VMEM),
        cost_estimate=pl.CostEstimate(flops=flops, bytes_accessed=size, transcendentals=0),
    )(*args)


def swap(block, axis):
    return lax.all_to_all(block, axis, split_axis=0, concat_axis=0, tiled=True)


def per_device(table, values, gates, cotangent, filters, skip_gain):
    shape = functools.partial(jax.ShapeDtypeStruct, dtype=jnp.bfloat16)
    spectrum = jax.ShapeDtypeStruct((2 * WIDTH, WIDTH), jnp.float32)
    packed = shape((BLOCKS, 5 * MINE, 128))
    ctx_half = (lax.axis_index("ctx") // HALF).astype(jnp.int32).reshape(1)
    mp_place = lax.axis_index("mp").astype(jnp.int32).reshape(1)
    skip_rows = jnp.broadcast_to(skip_gain[None, :], (8, WIDTH))
    cube = 2 * WIDTH**3

    block = call(
        outgoing_kernel, (packed,), (mp_place, values, gates, cotangent, filters.T),
        2 * cube, scalars=1, fetched=True,
    )
    block = swap(block, "ctx")
    value, gated, own, sent = call(
        spectra_kernel,
        (spectrum, spectrum, shape((BLOCKS, WIDTH)), shape((SHARDS, BLOCKS, WIDTH))),
        (ctx_half, mp_place, block, table["first"], table["middle"], table["last_by_channel"], table["twist"]),
        18 * cube, scalars=2,
    )
    sent = swap(sent, "mp")
    block = call(
        results_kernel, (packed,),
        (ctx_half, mp_place, sent, own, value, gated, table["first_by_channel"], table["middle"], table["last"], table["twist"]),
        18 * cube, scalars=2,
    )
    block = swap(block, "ctx")
    grad_gates, grad_values, grad_filters = call(
        finished_kernel, (shape(values.shape), shape(values.shape), shape((HALF, WIDTH))),
        (mp_place, block, values, gates, cotangent, skip_rows), 2 * cube, scalars=1,
    )
    return (grad_gates, grad_values, grad_filters.T)


def solution(mesh):
    return jax.shard_map(
        functools.partial(per_device, tables()),
        mesh=mesh,
        in_specs=(P("ctx", "mp"), P("ctx", "mp"), P("ctx", "mp"), P("ctx", "mp"), P("mp")),
        out_specs=(P("ctx", "mp"), P("ctx", "mp"), P("ctx", "mp")),
        check_vma=False,
    )
```

```python
import functools
import math

import jax
import jax.numpy as jnp
import numpy as np
from jax import lax
from jax.experimental import pallas as pl
from jax.experimental.pallas import tpu as pltpu
from jax.sharding import PartitionSpec as P

BLOCKS = 32
HALF = 16
MINE = 8
WIDTH = 256
LENGTH = BLOCKS * WIDTH
SHARDS = 16
FACTOR = 1.0 / math.sqrt(LENGTH)
VMEM = 32 * 1024 * 1024
MOST = 63 * 1024 * 1024


def tables():
    quarter = np.arange(BLOCKS) + 0.25
    outer = 2.0 * np.pi * np.outer(quarter, np.arange(BLOCKS)) / BLOCKS
    eye = np.eye(MINE)
    cos_rows = np.kron(np.cos(outer), eye)
    sin_rows = np.kron(np.sin(outer), eye)
    first = np.concatenate([cos_rows, -sin_rows], 0)
    last = np.concatenate([cos_rows.T, sin_rows.T], 1)
    by_channel = np.arange(BLOCKS * MINE).reshape(BLOCKS, MINE).T.reshape(-1)
    inner = 2.0 * np.pi * (np.outer(np.arange(WIDTH), np.arange(WIDTH)) % WIDTH) / WIDTH
    cos_in, sin_in = (np.cos(inner), np.sin(inner))
    twist = 2.0 * np.pi * np.outer(quarter, np.arange(WIDTH)) / LENGTH
    low = lambda array: array.astype(np.float32).astype(jnp.bfloat16)
    return dict(
        first=low(first),
        first_by_channel=low(first[:, by_channel]),
        middle=low(np.concatenate([cos_in, sin_in], 1)),
        last=low(last),
        last_by_channel=low(last[by_channel]),
        twist=np.stack([np.cos(twist), np.sin(twist)]).astype(np.float32),
    )


def dot(left, right, dims=((1,), (0,))):
    return lax.dot_general(
        left.astype(jnp.bfloat16),
        right.astype(jnp.bfloat16),
        (dims, ((), ())),
        preferred_element_type=jnp.float32,
    )


def source_of(half, row, place):
    return jnp.where(row == 0, 8 * half + (place & 7), (place - row - 8 * half) & 15)


def order_of(place):
    row = lax.broadcasted_iota(jnp.int32, (WIDTH, WIDTH), 0)
    channel = lax.broadcasted_iota(jnp.int32, (WIDTH, WIDTH), 1)
    wanted = 16 * source_of(row >> 7, row & 7, place) + ((row >> 3) & 15)
    return (channel == wanted).astype(jnp.float32).astype(jnp.bfloat16)


def whirl(both, middle, twist_first, twist):
    if twist_first:
        both = twisted(both, twist)
    terms = dot(both, middle)
    real, imag = (terms[:WIDTH], terms[WIDTH:])
    both = jnp.concatenate(
        [real[:, :WIDTH] + imag[:, WIDTH:], imag[:, :WIDTH] - real[:, WIDTH:]], 0
    )
    return both if twist_first else twisted(both, twist)


def twisted(both, twist):
    shape = (BLOCKS, MINE, WIDTH)
    cos, sin = (twist[0][:, None, :], twist[1][:, None, :])
    real, imag = (both[:WIDTH].reshape(shape), both[WIDTH:].reshape(shape))
    both = jnp.concatenate([real * cos + imag * sin, imag * cos - real * sin], 0)
    return both.reshape(2 * WIDTH, WIDTH)


def forward(rows, first, middle, twist):
    return whirl(dot(first, rows), middle, True, twist)


def inverse(real, imag, middle, last, twist):
    return dot(last, whirl(jnp.concatenate([real, imag], 0), middle, False, twist))


def parts_of(spectrum):
    return (spectrum[:WIDTH], spectrum[WIDTH:])


def pack(upper, lower, extra):
    pieces = []
    for rows in (upper, lower):
        rows = rows.reshape(BLOCKS, MINE, WIDTH)
        pieces += [rows[:, at : at + 2, :] for at in range(0, MINE, 2)]
    spread = [piece[:, None, :] for piece in (extra[:, :128], extra[:, 128:])]
    pieces.append(jnp.concatenate(spread, 1))
    return jnp.concatenate(pieces, 2).astype(jnp.bfloat16)


def rows_of(block, at):
    start = 4 * WIDTH * at
    block = block[:, :, start : start + 4 * WIDTH].astype(jnp.float32)
    rows = jnp.concatenate([block[:, :, k * WIDTH : (k + 1) * WIDTH] for k in range(4)], 1)
    return rows.reshape(BLOCKS * MINE, WIDTH)


def extra_of(block):
    block = block[:, :, 8 * WIDTH :].astype(jnp.float32)
    return jnp.concatenate([block[:, 0], block[:, 1]], 1)


def product_of(cotangent, gates):
    return (cotangent.astype(jnp.float32) * gates.astype(jnp.float32)).astype(jnp.bfloat16)


def outgoing(order, values, gates, cotangent, filters):
    gated = product_of(cotangent, gates)
    across = ((1,), (1,))
    twice = jnp.concatenate([filters, filters], 0).astype(jnp.float32)
    return pack(dot(order, values, across), dot(order, gated, across), twice)


def spectra(block, first, middle, last_by_channel, twist):
    value = forward(rows_of(block, 0), first, middle, twist)
    gated = forward(rows_of(block, 1), first, middle, twist)
    (value_r, value_i), (gated_r, gated_i) = (parts_of(value), parts_of(gated))
    lagged = inverse(
        gated_r * value_r + gated_i * value_i,
        gated_r * value_i - gated_i * value_r,
        middle, last_by_channel, twist,
    ) * (1.0 / LENGTH)
    lagged = lagged.reshape(MINE, BLOCKS, WIDTH)
    return (value, gated, lagged.astype(jnp.bfloat16), extra_of(block).astype(jnp.bfloat16))


def results(filters, total, value, gated, first_by_channel, middle, last, twist):
    filt = forward(filters.reshape(MINE * BLOCKS, WIDTH), first_by_channel, middle, twist)
    (filt_r, filt_i) = parts_of(filt)
    (value_r, value_i), (gated_r, gated_i) = (parts_of(value), parts_of(gated))
    scale = FACTOR / LENGTH
    conv = inverse(
        filt_r * value_r - filt_i * value_i,
        -filt_r * value_i - filt_i * value_r,
        middle, last, twist,
    ) * scale
    back = inverse(
        filt_r * gated_r + filt_i * gated_i,
        filt_i * gated_r - filt_r * gated_i,
        middle, last, twist,
    ) * scale
    return pack(conv, back, total * FACTOR)


def finished(place, block, values, gates, cotangent, skip_rows):
    down = ((0,), (0,))
    order = order_of(place)
    conv = dot(rows_of(block, 0), order, down)
    back = dot(rows_of(block, 1), order, down)
    gated = product_of(cotangent, gates).astype(jnp.float32)
    grad_gates = cotangent.astype(jnp.float32) * (conv + skip_rows[:1] * values.astype(jnp.float32))
    grad_values = back + skip_rows[:1] * gated
    partial = extra_of(block)
    grad_filters = partial[:HALF] + partial[HALF:]
    return tuple(out.astype(jnp.bfloat16) for out in (grad_gates, grad_values, grad_filters))


def outgoing_kernel(mp_place, values, gates, cotangent, filters, out, *scratch):
    held, sems = (scratch[:-1], scratch[-1])
    copies = []
    for at, (source, target) in enumerate(zip((values, gates, cotangent, filters), held)):
        copies.append(pltpu.make_async_copy(source, target, sems.at[at]))
        copies[-1].start()
    order = order_of(mp_place[0])
    for copy in copies:
        copy.wait()
    out[...] = outgoing(order, *(ref[...] for ref in held))


def spectra_kernel(ctx_half, mp_place, *refs):
    half, place = (ctx_half[0], mp_place[0])
    value, gated, own, sent = refs[-4:]
    value[...], gated[...], lagged, own_rows = spectra(*(ref[...] for ref in refs[:-4]))
    own[...] = own_rows
    sent[...] = jnp.broadcast_to(own_rows[None], sent.shape)
    for row in range(MINE):
        sent[source_of(half, row, place)] = lagged[row]


def results_kernel(ctx_half, mp_place, arrived, own, *refs):
    half, place = (ctx_half[0], mp_place[0])
    held = source_of(half, 0, place) == place
    filters = [jnp.where(held, own[...], arrived[source_of(half, 0, place)])]
    filters += [arrived[source_of(half, row, place)] for row in range(1, MINE)]
    total = jnp.zeros((BLOCKS, WIDTH), jnp.float32)
    for other in range(SHARDS):
        ahead = (other - place) & 15
        near = (ahead >= 1) & (ahead <= 7) | (place == other & 7)
        total += jnp.where(near == (half == 0), arrived[other].astype(jnp.float32), 0.0)
    refs[-1][...] = results(jnp.stack(filters), total, *(ref[...] for ref in refs[:-1]))


def finished_kernel(mp_place, *refs):
    outs = finished(mp_place[0], *(ref[...] for ref in refs[:-3]))
    for ref, out in zip(refs[-3:], outs):
        ref[...] = out


def call(kernel, outs, args, flops, scalars=0, fetched=False):
    whole = pl.BlockSpec(memory_space=pltpu.VMEM)
    scalar = pl.BlockSpec(memory_space=pltpu.SMEM)
    given = pl.BlockSpec(memory_space=pl.ANY) if fetched else whole
    size = sum(math.prod(out.shape) * out.dtype.itemsize for out in (*outs, *args))
    single = len(outs) == 1
    scratch = []
    if fetched:
        scratch = [pltpu.VMEM(arg.shape, arg.dtype) for arg in args[scalars:]]
        scratch.append(pltpu.SemaphoreType.DMA((len(scratch),)))
    return pl.pallas_call(
        kernel,
        out_shape=outs[0] if single else outs,
        in_specs=[scalar] * scalars + [given] * (len(args) - scalars),
        out_specs=whole if single else (whole,) * len(outs),
        scratch_shapes=scratch,
        compiler_params=pltpu.CompilerParams(vmem_limit_bytes=MOST if fetched else VMEM),
        cost_estimate=pl.CostEstimate(flops=flops, bytes_accessed=size, transcendentals=0),
    )(*args)


def swap(block, axis):
    return lax.all_to_all(block, axis, split_axis=0, concat_axis=0, tiled=True)


def per_device(table, values, gates, cotangent, filters, skip_gain):
    shape = functools.partial(jax.ShapeDtypeStruct, dtype=jnp.bfloat16)
    spectrum = jax.ShapeDtypeStruct((2 * WIDTH, WIDTH), jnp.float32)
    packed = shape((BLOCKS, 2, 8 * WIDTH + 128))
    ctx_half = (lax.axis_index("ctx") // HALF).astype(jnp.int32).reshape(1)
    mp_place = lax.axis_index("mp").astype(jnp.int32).reshape(1)
    skip_rows = jnp.broadcast_to(skip_gain[None, :], (8, WIDTH))
    cube = 2 * WIDTH**3

    block = call(
        outgoing_kernel, (packed,), (mp_place, values, gates, cotangent, filters.T),
        2 * cube, scalars=1, fetched=True,
    )
    block = swap(block, "ctx")
    value, gated, own, sent = call(
        spectra_kernel,
        (spectrum, spectrum, shape((BLOCKS, WIDTH)), shape((SHARDS, BLOCKS, WIDTH))),
        (ctx_half, mp_place, block, table["first"], table["middle"], table["last_by_channel"], table["twist"]),
        18 * cube, scalars=2,
    )
    sent = swap(sent, "mp")
    block = call(
        results_kernel, (packed,),
        (ctx_half, mp_place, sent, own, value, gated, table["first_by_channel"], table["middle"], table["last"], table["twist"]),
        18 * cube, scalars=2,
    )
    block = swap(block, "ctx")
    grad_gates, grad_values, grad_filters = call(
        finished_kernel, (shape(values.shape), shape(values.shape), shape((HALF, WIDTH))),
        (mp_place, block, values, gates, cotangent, skip_rows), 2 * cube, scalars=1,
    )
    return (grad_gates, grad_values, grad_filters.T)


def solution(mesh):
    return jax.shard_map(
        functools.partial(per_device, tables()),
        mesh=mesh,
        in_specs=(P("ctx", "mp"), P("ctx", "mp"), P("ctx", "mp"), P("ctx", "mp"), P("mp")),
        out_specs=(P("ctx", "mp"), P("ctx", "mp"), P("ctx", "mp")),
        check_vma=False,
    )
```

```python
import functools
import math

import jax
import jax.numpy as jnp
import numpy as np
from jax import lax
from jax.experimental import pallas as pl
from jax.experimental.pallas import tpu as pltpu
from jax.sharding import PartitionSpec as P

BLOCKS = 32
HALF = 16
MINE = 8
WIDTH = 256
LENGTH = BLOCKS * WIDTH
SHARDS = 16
FACTOR = 1.0 / math.sqrt(LENGTH)
VMEM = 32 * 1024 * 1024


def tables():
    quarter = np.arange(BLOCKS) + 0.25
    outer = 2.0 * np.pi * np.outer(quarter, np.arange(BLOCKS)) / BLOCKS
    eye = np.eye(MINE)
    cos_rows = np.kron(np.cos(outer), eye)
    sin_rows = np.kron(np.sin(outer), eye)
    first = np.concatenate([cos_rows, -sin_rows], 0)
    last = np.concatenate([cos_rows.T, sin_rows.T], 1)
    by_channel = np.arange(BLOCKS * MINE).reshape(BLOCKS, MINE).T.reshape(-1)
    inner = 2.0 * np.pi * (np.outer(np.arange(WIDTH), np.arange(WIDTH)) % WIDTH) / WIDTH
    cos_in, sin_in = (np.cos(inner), np.sin(inner))
    twist = 2.0 * np.pi * np.outer(quarter, np.arange(WIDTH)) / LENGTH
    low = lambda array: array.astype(np.float32).astype(jnp.bfloat16)
    return dict(
        first=low(first),
        first_by_channel=low(first[:, by_channel]),
        middle=low(np.block([[cos_in, -sin_in], [sin_in, cos_in]])),
        last=low(last),
        last_by_channel=low(last[by_channel]),
        twist=np.stack([np.cos(twist), np.sin(twist)]).astype(np.float32),
    )


def dot(left, right, dims=((1,), (0,))):
    return lax.dot_general(
        left.astype(jnp.bfloat16),
        right.astype(jnp.bfloat16),
        (dims, ((), ())),
        preferred_element_type=jnp.float32,
    )


def source_of(half, row, place):
    return jnp.where(row == 0, 8 * half + (place & 7), (place - row - 8 * half) & 15)


def order_of(place):
    row = lax.broadcasted_iota(jnp.int32, (WIDTH, WIDTH), 0)
    channel = lax.broadcasted_iota(jnp.int32, (WIDTH, WIDTH), 1)
    wanted = 16 * source_of(row >> 7, row & 7, place) + ((row >> 3) & 15)
    return (channel == wanted).astype(jnp.float32).astype(jnp.bfloat16)


def twisted(real, imag, twist):
    shape = (BLOCKS, MINE, WIDTH)
    cos, sin = (twist[0][:, None, :], twist[1][:, None, :])
    real, imag = (real.reshape(shape), imag.reshape(shape))
    both = [real * cos + imag * sin, imag * cos - real * sin]
    return [part.reshape(WIDTH, WIDTH) for part in both]


def cut(array, step, axis):
    return [lax.slice_in_dim(array, at, at + step, axis=axis) for at in range(0, array.shape[axis], step)]


def forward(signals, first, middle, twist):
    both = [cut(part, WIDTH, 0) for part in cut(dot(first, jnp.concatenate(signals, 1)), WIDTH, 1)]
    both = [jnp.concatenate(twisted(*parts, twist), 1) for parts in both]
    return cut(dot(jnp.concatenate(both, 0), middle), WIDTH, 0)


def inverse(spectra, middle, last, twist):
    both = jnp.concatenate([jnp.concatenate(parts, 1) for parts in spectra], 0)
    both = [cut(part, WIDTH, 1) for part in cut(dot(both, middle), WIDTH, 0)]
    both = [jnp.concatenate(twisted(*parts, twist), 0) for parts in both]
    return cut(dot(last, jnp.concatenate(both, 1)), WIDTH, 1)


def parts_of(spectrum):
    return (spectrum[:, :WIDTH], spectrum[:, WIDTH:])


def pack(upper, lower, extra):
    pieces = []
    for rows in (upper, lower):
        rows = rows.reshape(BLOCKS, MINE, WIDTH)
        pieces += [rows[:, at : at + 2, :] for at in range(0, MINE, 2)]
    spread = [piece[:, None, :] for piece in (extra[:, :128], extra[:, 128:])]
    pieces.append(jnp.concatenate(spread, 1))
    return jnp.concatenate(pieces, 2).astype(jnp.bfloat16)


def rows_of(block, at):
    start = 4 * WIDTH * at
    block = block[:, :, start : start + 4 * WIDTH].astype(jnp.float32)
    rows = jnp.concatenate([block[:, :, k * WIDTH : (k + 1) * WIDTH] for k in range(4)], 1)
    return rows.reshape(BLOCKS * MINE, WIDTH)


def extra_of(block):
    block = block[:, :, 8 * WIDTH :].astype(jnp.float32)
    return jnp.concatenate([block[:, 0], block[:, 1]], 1)


def product_of(cotangent, gates):
    return (cotangent.astype(jnp.float32) * gates.astype(jnp.float32)).astype(jnp.bfloat16)


def packed_rows(order, signal):
    return dot(order, signal, ((1,), (1,)))


def spectra(block, first, middle, last_by_channel, twist):
    value, gated = forward([rows_of(block, 0), rows_of(block, 1)], first, middle, twist)
    (value_r, value_i), (gated_r, gated_i) = (parts_of(value), parts_of(gated))
    lag_spec = (gated_r * value_r + gated_i * value_i, gated_r * value_i - gated_i * value_r)
    (lagged,) = inverse([lag_spec], middle, last_by_channel, twist)
    lagged = (lagged * (1.0 / LENGTH)).reshape(MINE, BLOCKS, WIDTH)
    return (value, gated, lagged.astype(jnp.bfloat16), extra_of(block).astype(jnp.bfloat16))


def results(filters, total, value, gated, first_by_channel, middle, last, twist):
    (filt,) = forward([filters.reshape(MINE * BLOCKS, WIDTH)], first_by_channel, middle, twist)
    (filt_r, filt_i) = parts_of(filt)
    (value_r, value_i), (gated_r, gated_i) = (parts_of(value), parts_of(gated))
    conv_spec = (filt_r * value_r - filt_i * value_i, -filt_r * value_i - filt_i * value_r)
    back_spec = (filt_r * gated_r + filt_i * gated_i, filt_i * gated_r - filt_r * gated_i)
    conv, back = inverse([conv_spec, back_spec], middle, last, twist)
    scale = FACTOR / LENGTH
    return pack(conv * scale, back * scale, total * FACTOR)


def finished(place, block, values, gates, cotangent, skip_rows):
    down = ((0,), (0,))
    order = order_of(place)
    conv = dot(rows_of(block, 0), order, down)
    back = dot(rows_of(block, 1), order, down)
    gated = product_of(cotangent, gates).astype(jnp.float32)
    grad_gates = cotangent.astype(jnp.float32) * (conv + skip_rows[:1] * values.astype(jnp.float32))
    grad_values = back + skip_rows[:1] * gated
    partial = extra_of(block)
    grad_filters = partial[:HALF] + partial[HALF:]
    return tuple(out.astype(jnp.bfloat16) for out in (grad_gates, grad_values, grad_filters))


def outgoing_kernel(place, values, gates, cotangent, filters, out, *scratch):
    held, sems = (scratch[:-1], scratch[-1])
    copies = []
    for at, (source, target) in enumerate(zip((values, gates, cotangent, filters), held)):
        copies.append(pltpu.make_async_copy(source, target, sems.at[at]))
        copies[-1].start()
    order = order_of(place[0] & 15)
    for copy in copies:
        copy.wait()
    value_rows = packed_rows(order, held[0][...])
    gated_rows = packed_rows(order, product_of(held[2][...], held[1][...]))
    filter_rows = jnp.concatenate([held[3][...]] * 2, 0).astype(jnp.float32)
    out[...] = pack(value_rows, gated_rows, filter_rows)


def spectra_kernel(place, *refs):
    half, place = (place[0] >> 4, place[0] & 15)
    value, gated, own, sent = refs[-4:]
    value[...], gated[...], lagged, own_rows = spectra(*(ref[...] for ref in refs[:-4]))
    own[...] = own_rows
    sent[...] = jnp.broadcast_to(own_rows[None], sent.shape)
    for row in range(MINE):
        sent[source_of(half, row, place)] = lagged[row]


def results_kernel(place, arrived, own, *refs):
    half, place = (place[0] >> 4, place[0] & 15)
    held = source_of(half, 0, place) == place
    filters = [jnp.where(held, own[...], arrived[source_of(half, 0, place)])]
    filters += [arrived[source_of(half, row, place)] for row in range(1, MINE)]
    total = jnp.zeros((BLOCKS, WIDTH), jnp.float32)
    for other in range(SHARDS):
        ahead = (other - place) & 15
        near = (ahead >= 1) & (ahead <= 7) | (place == other & 7)
        total += jnp.where(near == (half == 0), arrived[other].astype(jnp.float32), 0.0)
    refs[-1][...] = results(jnp.stack(filters), total, *(ref[...] for ref in refs[:-1]))


def finished_kernel(place, *refs):
    outs = finished(place[0] & 15, *(ref[...] for ref in refs[:-3]))
    for ref, out in zip(refs[-3:], outs):
        ref[...] = out


def call(kernel, outs, args, flops, scalars=0, fetched=False):
    whole = pl.BlockSpec(memory_space=pltpu.VMEM)
    scalar = pl.BlockSpec(memory_space=pltpu.SMEM)
    given = pl.BlockSpec(memory_space=pl.ANY) if fetched else whole
    size = sum(math.prod(out.shape) * out.dtype.itemsize for out in (*outs, *args))
    single = len(outs) == 1
    scratch = []
    if fetched:
        args = (*args[:scalars], *(pltpu.with_memory_space_constraint(arg, pltpu.HBM) for arg in args[scalars:]))
        scratch = [pltpu.VMEM(arg.shape, arg.dtype) for arg in args[scalars:]]
        scratch.append(pltpu.SemaphoreType.DMA((len(scratch),)))
    return pl.pallas_call(
        kernel,
        out_shape=outs[0] if single else outs,
        in_specs=[scalar] * scalars + [given] * (len(args) - scalars),
        out_specs=whole if single else (whole,) * len(outs),
        scratch_shapes=scratch,
        compiler_params=pltpu.CompilerParams(vmem_limit_bytes=VMEM),
        cost_estimate=pl.CostEstimate(flops=flops, bytes_accessed=size, transcendentals=0),
    )(*args)


def swap(block, axis):
    return lax.all_to_all(block, axis, split_axis=0, concat_axis=0, tiled=True)


def per_device(table, values, gates, cotangent, filters, skip_gain):
    shape = functools.partial(jax.ShapeDtypeStruct, dtype=jnp.bfloat16)
    spectrum = jax.ShapeDtypeStruct((WIDTH, 2 * WIDTH), jnp.float32)
    packed = shape((BLOCKS, 2, 8 * WIDTH + 128))
    place = (lax.axis_index("ctx") // HALF * SHARDS + lax.axis_index("mp")).astype(jnp.int32).reshape(1)
    skip_rows = jnp.broadcast_to(skip_gain[None, :], (8, WIDTH))
    cube = 2 * WIDTH**3

    block = call(
        outgoing_kernel, (packed,), (place, values, gates, cotangent, filters.T),
        2 * cube, scalars=1, fetched=True,
    )
    block = swap(block, "ctx")
    value, gated, own, sent = call(
        spectra_kernel,
        (spectrum, spectrum, shape((BLOCKS, WIDTH)), shape((SHARDS, BLOCKS, WIDTH))),
        (place, block, table["first"], table["middle"], table["last_by_channel"], table["twist"]),
        18 * cube, scalars=1,
    )
    sent = swap(sent, "mp")
    block = call(
        results_kernel, (packed,),
        (place, sent, own, value, gated, table["first_by_channel"], table["middle"], table["last"], table["twist"]),
        18 * cube, scalars=1,
    )
    block = swap(block, "ctx")
    grad_gates, grad_values, grad_filters = call(
        finished_kernel, (shape(values.shape), shape(values.shape), shape((HALF, WIDTH))),
        (place, block, values, gates, cotangent, skip_rows), 2 * cube, scalars=1,
    )
    return (grad_gates, grad_values, grad_filters.T)


def solution(mesh):
    return jax.shard_map(
        functools.partial(per_device, tables()),
        mesh=mesh,
        in_specs=(P("ctx", "mp"), P("ctx", "mp"), P("ctx", "mp"), P("ctx", "mp"), P("mp")),
        out_specs=(P("ctx", "mp"), P("ctx", "mp"), P("ctx", "mp")),
        check_vma=False,
    )
```

```python
import functools
import math

import jax
import jax.numpy as jnp
import numpy as np
from jax import lax
from jax.experimental import pallas as pl
from jax.experimental.pallas import tpu as pltpu
from jax.sharding import PartitionSpec as P

BLOCKS = 32
HALF = 16
MINE = 8
WIDTH = 256
LENGTH = BLOCKS * WIDTH
SHARDS = 16
ORDER = tuple(HALF * x + z for z in (8, 9, 10, 15, 11, 14, 12, 7, 6, 13, 4, 5, 3, 2, 1, 0) for x in (0, 1))
LATER = sum(1 << device for device in ORDER[HALF:])
FACTOR = 1.0 / math.sqrt(LENGTH)
VMEM = 32 * 1024 * 1024


def tables():
    quarter = np.arange(BLOCKS) + 0.25
    outer = 2.0 * np.pi * np.outer(quarter, ORDER) / BLOCKS
    eye = np.eye(MINE)
    cos_rows = np.kron(np.cos(outer), eye)
    sin_rows = np.kron(np.sin(outer), eye)
    first = np.concatenate([cos_rows, -sin_rows], 0)
    last = np.concatenate([cos_rows.T, sin_rows.T], 1)
    by_channel = np.arange(BLOCKS * MINE).reshape(BLOCKS, MINE).T.reshape(-1)
    inner = 2.0 * np.pi * (np.outer(np.arange(WIDTH), np.arange(WIDTH)) % WIDTH) / WIDTH
    cos_in, sin_in = (np.cos(inner), np.sin(inner))
    twist = 2.0 * np.pi * np.outer(quarter, np.arange(WIDTH)) / LENGTH
    low = lambda array: array.astype(np.float32).astype(jnp.bfloat16)
    return dict(
        first=low(first),
        first_by_channel=low(first[:, by_channel]),
        middle=low(np.block([[cos_in, -sin_in], [sin_in, cos_in]])),
        last=low(last),
        last_by_channel=low(last[by_channel]),
        twist=np.stack([np.cos(twist), np.sin(twist)]).astype(np.float32),
    )


def dot(left, right, dims=((1,), (0,))):
    return lax.dot_general(
        left.astype(jnp.bfloat16),
        right.astype(jnp.bfloat16),
        (dims, ((), ())),
        preferred_element_type=jnp.float32,
    )


def source_of(half, row, place):
    return jnp.where(row == 0, 8 * half + (place & 7), (place - row - 8 * half) & 15)


def order_of(place):
    row = lax.broadcasted_iota(jnp.int32, (WIDTH, WIDTH), 0)
    channel = lax.broadcasted_iota(jnp.int32, (WIDTH, WIDTH), 1)
    wanted = 16 * source_of(row >> 7, row & 7, place) + ((row >> 3) & 15)
    return (channel == wanted).astype(jnp.float32).astype(jnp.bfloat16)


def twisted(real, imag, twist):
    shape = (BLOCKS, MINE, WIDTH)
    cos, sin = (twist[0][:, None, :], twist[1][:, None, :])
    real, imag = (real.reshape(shape), imag.reshape(shape))
    both = [real * cos + imag * sin, imag * cos - real * sin]
    return [part.reshape(WIDTH, WIDTH) for part in both]


def cut(array, step, axis):
    return [lax.slice_in_dim(array, at, at + step, axis=axis) for at in range(0, array.shape[axis], step)]


def forward(signals, first, middle, twist):
    both = [cut(part, WIDTH, 0) for part in cut(dot(first, jnp.concatenate(signals, 1)), WIDTH, 1)]
    both = [jnp.concatenate(twisted(*parts, twist), 1) for parts in both]
    return cut(dot(jnp.concatenate(both, 0), middle), WIDTH, 0)


def inverse(spectra, middle, last, twist):
    both = jnp.concatenate([jnp.concatenate(parts, 1) for parts in spectra], 0)
    both = [cut(part, WIDTH, 1) for part in cut(dot(both, middle), WIDTH, 0)]
    both = [jnp.concatenate(twisted(*parts, twist), 0) for parts in both]
    return cut(dot(last, jnp.concatenate(both, 1)), WIDTH, 1)


def parts_of(spectrum):
    return (spectrum[:, :WIDTH], spectrum[:, WIDTH:])


def pack(upper, lower, extra):
    pieces = []
    for rows in (upper, lower):
        rows = rows.reshape(BLOCKS, MINE, WIDTH)
        pieces += [rows[:, at : at + 2, :] for at in range(0, MINE, 2)]
    spread = [piece[:, None, :] for piece in (extra[:, :128], extra[:, 128:])]
    pieces.append(jnp.concatenate(spread, 1))
    return jnp.concatenate(pieces, 2).astype(jnp.bfloat16)


def rows_of(block, at):
    start = 4 * WIDTH * at
    block = block[:, :, start : start + 4 * WIDTH].astype(jnp.float32)
    rows = jnp.concatenate([block[:, :, k * WIDTH : (k + 1) * WIDTH] for k in range(4)], 1)
    return rows.reshape(BLOCKS * MINE, WIDTH)


def extra_of(block):
    block = block[:, :, 8 * WIDTH :].astype(jnp.float32)
    return jnp.concatenate([block[:, 0], block[:, 1]], 1)


def product_of(cotangent, gates):
    return (cotangent.astype(jnp.float32) * gates.astype(jnp.float32)).astype(jnp.bfloat16)


def packed_rows(order, signal):
    return dot(order, signal, ((1,), (1,)))


def spectra(block, first, middle, last_by_channel, twist):
    value, gated = forward([rows_of(block, 0), rows_of(block, 1)], first, middle, twist)
    (value_r, value_i), (gated_r, gated_i) = (parts_of(value), parts_of(gated))
    lag_spec = (gated_r * value_r + gated_i * value_i, gated_r * value_i - gated_i * value_r)
    (lagged,) = inverse([lag_spec], middle, last_by_channel, twist)
    lagged = (lagged * (1.0 / LENGTH)).reshape(MINE, BLOCKS, WIDTH)
    return (value, gated, lagged.astype(jnp.bfloat16), extra_of(block).astype(jnp.bfloat16))


def results(filters, total, value, gated, first_by_channel, middle, last, twist):
    (filt,) = forward([filters.reshape(MINE * BLOCKS, WIDTH)], first_by_channel, middle, twist)
    (filt_r, filt_i) = parts_of(filt)
    (value_r, value_i), (gated_r, gated_i) = (parts_of(value), parts_of(gated))
    conv_spec = (filt_r * value_r - filt_i * value_i, -filt_r * value_i - filt_i * value_r)
    back_spec = (filt_r * gated_r + filt_i * gated_i, filt_i * gated_r - filt_r * gated_i)
    conv, back = inverse([conv_spec, back_spec], middle, last, twist)
    scale = FACTOR / LENGTH
    return pack(conv * scale, back * scale, total * FACTOR)


def finished(place, block, values, gates, cotangent, skip_rows):
    down = ((0,), (0,))
    order = order_of(place)
    conv = dot(rows_of(block, 0), order, down)
    back = dot(rows_of(block, 1), order, down)
    gated = product_of(cotangent, gates).astype(jnp.float32)
    grad_gates = cotangent.astype(jnp.float32) * (conv + skip_rows[:1] * values.astype(jnp.float32))
    grad_values = back + skip_rows[:1] * gated
    partial = extra_of(block)
    grad_filters = partial[:HALF] + partial[HALF:]
    return tuple(out.astype(jnp.bfloat16) for out in (grad_gates, grad_values, grad_filters))


def outgoing_kernel(place, values, gates, cotangent, filters, out, *scratch):
    held, sems = (scratch[:-1], scratch[-1])
    copies = []
    for at, (source, target) in enumerate(zip((values, gates, cotangent, filters), held)):
        copies.append(pltpu.make_async_copy(source, target, sems.at[at]))
        copies[-1].start()
    order = order_of(place[0] & 15)
    for copy in copies:
        copy.wait()
    value_rows = packed_rows(order, held[0][...])
    gated_rows = packed_rows(order, product_of(held[2][...], held[1][...]))
    filter_rows = jnp.concatenate([held[3][...]] * 2, 0).astype(jnp.float32)
    out[...] = pack(value_rows, gated_rows, filter_rows)


def spectra_kernel(place, *refs):
    half, place = (place[0] >> 4, place[0] & 15)
    value, gated, own, sent = refs[-4:]
    value[...], gated[...], lagged, own_rows = spectra(*(ref[...] for ref in refs[:-4]))
    own[...] = own_rows
    sent[...] = jnp.broadcast_to(own_rows[None], sent.shape)
    for row in range(MINE):
        sent[source_of(half, row, place)] = lagged[row]


def results_kernel(place, arrived, own, *refs):
    half, place = (place[0] >> 4, place[0] & 15)
    held = source_of(half, 0, place) == place
    filters = [jnp.where(held, own[...], arrived[source_of(half, 0, place)])]
    filters += [arrived[source_of(half, row, place)] for row in range(1, MINE)]
    total = jnp.zeros((BLOCKS, WIDTH), jnp.float32)
    for other in range(SHARDS):
        ahead = (other - place) & 15
        near = (ahead >= 1) & (ahead <= 7) | (place == other & 7)
        total += jnp.where(near == (half == 0), arrived[other].astype(jnp.float32), 0.0)
    refs[-1][...] = results(jnp.stack(filters), total, *(ref[...] for ref in refs[:-1]))


def finished_kernel(place, *refs):
    outs = finished(place[0] & 15, *(ref[...] for ref in refs[:-3]))
    for ref, out in zip(refs[-3:], outs):
        ref[...] = out


def call(kernel, outs, args, flops, scalars=0, fetched=False):
    whole = pl.BlockSpec(memory_space=pltpu.VMEM)
    scalar = pl.BlockSpec(memory_space=pltpu.SMEM)
    given = pl.BlockSpec(memory_space=pl.ANY) if fetched else whole
    size = sum(math.prod(out.shape) * out.dtype.itemsize for out in (*outs, *args))
    single = len(outs) == 1
    scratch = []
    if fetched:
        args = (*args[:scalars], *(pltpu.with_memory_space_constraint(arg, pltpu.HBM) for arg in args[scalars:]))
        scratch = [pltpu.VMEM(arg.shape, arg.dtype) for arg in args[scalars:]]
        scratch.append(pltpu.SemaphoreType.DMA((len(scratch),)))
    return pl.pallas_call(
        kernel,
        out_shape=outs[0] if single else outs,
        in_specs=[scalar] * scalars + [given] * (len(args) - scalars),
        out_specs=whole if single else (whole,) * len(outs),
        scratch_shapes=scratch,
        compiler_params=pltpu.CompilerParams(vmem_limit_bytes=VMEM),
        cost_estimate=pl.CostEstimate(flops=flops, bytes_accessed=size, transcendentals=0),
    )(*args)


def swap(block, axis, groups=None):
    return lax.all_to_all(block, axis, split_axis=0, concat_axis=0, tiled=True, axis_index_groups=groups)


def per_device(table, values, gates, cotangent, filters, skip_gain):
    shape = functools.partial(jax.ShapeDtypeStruct, dtype=jnp.bfloat16)
    spectrum = jax.ShapeDtypeStruct((WIDTH, 2 * WIDTH), jnp.float32)
    packed = shape((BLOCKS, 2, 8 * WIDTH + 128))
    later = lax.shift_right_logical(np.uint32(LATER), lax.axis_index("ctx").astype(jnp.uint32)) & 1
    place = (later.astype(jnp.int32) * SHARDS + lax.axis_index("mp")).reshape(1)
    skip_rows = jnp.broadcast_to(skip_gain[None, :], (8, WIDTH))
    cube = 2 * WIDTH**3

    block = call(
        outgoing_kernel, (packed,), (place, values, gates, cotangent, filters.T),
        2 * cube, scalars=1, fetched=True,
    )
    block = swap(block, "ctx", [ORDER])
    value, gated, own, sent = call(
        spectra_kernel,
        (spectrum, spectrum, shape((BLOCKS, WIDTH)), shape((SHARDS, BLOCKS, WIDTH))),
        (place, block, table["first"], table["middle"], table["last_by_channel"], table["twist"]),
        18 * cube, scalars=1,
    )
    sent = swap(sent, "mp")
    block = call(
        results_kernel, (packed,),
        (place, sent, own, value, gated, table["first_by_channel"], table["middle"], table["last"], table["twist"]),
        18 * cube, scalars=1,
    )
    block = swap(block, "ctx", [ORDER])
    grad_gates, grad_values, grad_filters = call(
        finished_kernel, (shape(values.shape), shape(values.shape), shape((HALF, WIDTH))),
        (place, block, values, gates, cotangent, skip_rows), 2 * cube, scalars=1,
    )
    return (grad_gates, grad_values, grad_filters.T)


def solution(mesh):
    return jax.shard_map(
        functools.partial(per_device, tables()),
        mesh=mesh,
        in_specs=(P("ctx", "mp"), P("ctx", "mp"), P("ctx", "mp"), P("ctx", "mp"), P("mp")),
        out_specs=(P("ctx", "mp"), P("ctx", "mp"), P("ctx", "mp")),
        check_vma=False,
    )
```

```python
import functools
import math

import jax
import jax.numpy as jnp
import numpy as np
from jax import lax
from jax.experimental import pallas as pl
from jax.experimental.pallas import tpu as pltpu
from jax.sharding import PartitionSpec as P

BLOCKS = 32
HALF = 16
MINE = 8
WIDTH = 256
LENGTH = BLOCKS * WIDTH
SHARDS = 16
ORDER = tuple(HALF * x + z for z in (8, 9, 10, 15, 11, 14, 12, 7, 6, 13, 4, 5, 3, 2, 1, 0) for x in (0, 1))
MP_ORDER = tuple(range(SHARDS))[::-1]
LATER = sum(1 << device for device in ORDER[HALF:])
FACTOR = 1.0 / math.sqrt(LENGTH)
VMEM = 32 * 1024 * 1024


def tables():
    quarter = np.arange(BLOCKS) + 0.25
    outer = 2.0 * np.pi * np.outer(quarter, ORDER) / BLOCKS
    eye = np.eye(MINE)
    cos_rows = np.kron(np.cos(outer), eye)
    sin_rows = np.kron(np.sin(outer), eye)
    first = np.concatenate([cos_rows, -sin_rows], 0)
    last = np.concatenate([cos_rows.T, sin_rows.T], 1)
    by_channel = np.arange(BLOCKS * MINE).reshape(BLOCKS, MINE).T.reshape(-1)
    inner = 2.0 * np.pi * (np.outer(np.arange(WIDTH), np.arange(WIDTH)) % WIDTH) / WIDTH
    cos_in, sin_in = (np.cos(inner), np.sin(inner))
    twist = 2.0 * np.pi * np.outer(quarter, np.arange(WIDTH)) / LENGTH
    low = lambda array: array.astype(np.float32).astype(jnp.bfloat16)
    return dict(
        first=low(first),
        first_by_channel=low(first[:, by_channel]),
        middle=low(np.block([[cos_in, -sin_in], [sin_in, cos_in]])),
        last=low(last),
        last_by_channel=low(last[by_channel]),
        twist=np.stack([np.cos(twist), np.sin(twist)]).astype(np.float32),
    )


def dot(left, right, dims=((1,), (0,))):
    return lax.dot_general(
        left.astype(jnp.bfloat16),
        right.astype(jnp.bfloat16),
        (dims, ((), ())),
        preferred_element_type=jnp.float32,
    )


def shard_at(place):
    return SHARDS - 1 - place


def source_of(half, row, place):
    return jnp.where(row == 0, 8 * half + (place & 7), (place - row - 8 * half) & 15)


def order_of(place):
    row = lax.broadcasted_iota(jnp.int32, (WIDTH, 1), 0)
    channel = lax.broadcasted_iota(jnp.int32, (WIDTH, WIDTH), 1)
    wanted = 16 * shard_at(source_of(row >> 7, row & 7, place)) + ((row >> 3) & 15)
    return (channel == wanted).astype(jnp.float32).astype(jnp.bfloat16)


def twisted(real, imag, twist):
    shape = (BLOCKS, MINE, WIDTH)
    cos, sin = (twist[0][:, None, :], twist[1][:, None, :])
    real, imag = (real.reshape(shape), imag.reshape(shape))
    both = [real * cos + imag * sin, imag * cos - real * sin]
    return [part.reshape(WIDTH, WIDTH) for part in both]


def cut(array, step, axis):
    return [lax.slice_in_dim(array, at, at + step, axis=axis) for at in range(0, array.shape[axis], step)]


def forward(signals, first, middle, twist):
    both = [cut(part, WIDTH, 0) for part in cut(dot(first, jnp.concatenate(signals, 1)), WIDTH, 1)]
    both = [jnp.concatenate(twisted(*parts, twist), 1) for parts in both]
    return cut(dot(jnp.concatenate(both, 0), middle), WIDTH, 0)


def inverse(spectra, middle, last, twist):
    both = jnp.concatenate([jnp.concatenate(parts, 1) for parts in spectra], 0)
    both = [cut(part, WIDTH, 1) for part in cut(dot(both, middle), WIDTH, 0)]
    both = [jnp.concatenate(twisted(*parts, twist), 0) for parts in both]
    return cut(dot(last, jnp.concatenate(both, 1)), WIDTH, 1)


def parts_of(spectrum):
    return (spectrum[:, :WIDTH], spectrum[:, WIDTH:])


def pack(upper, lower, extra):
    pieces = []
    for rows in (upper, lower):
        rows = rows.reshape(BLOCKS, MINE, WIDTH)
        pieces += [rows[:, at : at + 2, :] for at in range(0, MINE, 2)]
    spread = [piece[:, None, :] for piece in (extra[:, :128], extra[:, 128:])]
    pieces.append(jnp.concatenate(spread, 1))
    return jnp.concatenate(pieces, 2).astype(jnp.bfloat16)


def rows_of(block, at):
    start = 4 * WIDTH * at
    block = block[:, :, start : start + 4 * WIDTH].astype(jnp.float32)
    rows = jnp.concatenate([block[:, :, k * WIDTH : (k + 1) * WIDTH] for k in range(4)], 1)
    return rows.reshape(BLOCKS * MINE, WIDTH)


def extra_of(block):
    block = block[:, :, 8 * WIDTH :].astype(jnp.float32)
    return jnp.concatenate([block[:, 0], block[:, 1]], 1)


def product_of(cotangent, gates):
    return (cotangent.astype(jnp.float32) * gates.astype(jnp.float32)).astype(jnp.bfloat16)


def packed_rows(order, signal):
    return dot(order, signal, ((1,), (1,)))


def spectra(block, first, middle, last_by_channel, twist):
    value, gated = forward([rows_of(block, 0), rows_of(block, 1)], first, middle, twist)
    (value_r, value_i), (gated_r, gated_i) = (parts_of(value), parts_of(gated))
    lag_spec = (gated_r * value_r + gated_i * value_i, gated_r * value_i - gated_i * value_r)
    (lagged,) = inverse([lag_spec], middle, last_by_channel, twist)
    lagged = (lagged * (1.0 / LENGTH)).reshape(MINE, BLOCKS, WIDTH)
    return (value, gated, lagged.astype(jnp.bfloat16), extra_of(block).astype(jnp.bfloat16))


def results(filters, total, value, gated, first_by_channel, middle, last, twist):
    (filt,) = forward([filters.reshape(MINE * BLOCKS, WIDTH)], first_by_channel, middle, twist)
    (filt_r, filt_i) = parts_of(filt)
    (value_r, value_i), (gated_r, gated_i) = (parts_of(value), parts_of(gated))
    conv_spec = (filt_r * value_r - filt_i * value_i, -filt_r * value_i - filt_i * value_r)
    back_spec = (filt_r * gated_r + filt_i * gated_i, filt_i * gated_r - filt_r * gated_i)
    conv, back = inverse([conv_spec, back_spec], middle, last, twist)
    scale = FACTOR / LENGTH
    return pack(conv * scale, back * scale, total * FACTOR)


def finished(place, block, values, gates, cotangent, skip_rows):
    down = ((0,), (0,))
    order = order_of(place)
    conv = dot(rows_of(block, 0), order, down)
    back = dot(rows_of(block, 1), order, down)
    gated = product_of(cotangent, gates).astype(jnp.float32)
    grad_gates = cotangent.astype(jnp.float32) * (conv + skip_rows[:1] * values.astype(jnp.float32))
    grad_values = back + skip_rows[:1] * gated
    partial = extra_of(block)
    grad_filters = partial[:HALF] + partial[HALF:]
    return tuple(out.astype(jnp.bfloat16) for out in (grad_gates, grad_values, grad_filters))


def outgoing_kernel(place, values, gates, cotangent, filters, out, *scratch):
    held, sems = (scratch[:-1], scratch[-1])
    copies = []
    for at, (source, target) in enumerate(zip((values, gates, cotangent, filters), held)):
        copies.append(pltpu.make_async_copy(source, target, sems.at[at]))
        copies[-1].start()
    order = order_of(place[0] & 15)
    for copy in copies:
        copy.wait()
    value_rows = packed_rows(order, held[0][...])
    gated_rows = packed_rows(order, product_of(held[2][...], held[1][...]))
    filter_rows = jnp.concatenate([held[3][...]] * 2, 0).astype(jnp.float32)
    out[...] = pack(value_rows, gated_rows, filter_rows)


def spectra_kernel(place, *refs):
    half, place = (place[0] >> 4, place[0] & 15)
    value, gated, own, sent = refs[-4:]
    value[...], gated[...], lagged, own_rows = spectra(*(ref[...] for ref in refs[:-4]))
    own[...] = own_rows
    sent[...] = jnp.broadcast_to(own_rows[None], sent.shape)
    for row in range(MINE):
        sent[source_of(half, row, place)] = lagged[row]


def results_kernel(place, arrived, own, *refs):
    half, place = (place[0] >> 4, place[0] & 15)
    held = source_of(half, 0, place) == place
    filters = [jnp.where(held, own[...], arrived[source_of(half, 0, place)])]
    filters += [arrived[source_of(half, row, place)] for row in range(1, MINE)]
    total = jnp.zeros((BLOCKS, WIDTH), jnp.float32)
    for other in range(SHARDS):
        ahead = (other - place) & 15
        near = (ahead >= 1) & (ahead <= 7) | (place == other & 7)
        total += jnp.where(near == (half == 0), arrived[other].astype(jnp.float32), 0.0)
    refs[-1][...] = results(jnp.stack(filters), total, *(ref[...] for ref in refs[:-1]))


def finished_kernel(place, *refs):
    outs = finished(place[0] & 15, *(ref[...] for ref in refs[:-3]))
    for ref, out in zip(refs[-3:], outs):
        ref[...] = out


def call(kernel, outs, args, flops, scalars=0, fetched=False):
    whole = pl.BlockSpec(memory_space=pltpu.VMEM)
    scalar = pl.BlockSpec(memory_space=pltpu.SMEM)
    given = pl.BlockSpec(memory_space=pl.ANY) if fetched else whole
    size = sum(math.prod(out.shape) * out.dtype.itemsize for out in (*outs, *args))
    single = len(outs) == 1
    scratch = []
    if fetched:
        args = (*args[:scalars], *(pltpu.with_memory_space_constraint(arg, pltpu.HBM) for arg in args[scalars:]))
        scratch = [pltpu.VMEM(arg.shape, arg.dtype) for arg in args[scalars:]]
        scratch.append(pltpu.SemaphoreType.DMA((len(scratch),)))
    return pl.pallas_call(
        kernel,
        out_shape=outs[0] if single else outs,
        in_specs=[scalar] * scalars + [given] * (len(args) - scalars),
        out_specs=whole if single else (whole,) * len(outs),
        scratch_shapes=scratch,
        compiler_params=pltpu.CompilerParams(vmem_limit_bytes=VMEM),
        cost_estimate=pl.CostEstimate(flops=flops, bytes_accessed=size, transcendentals=0),
    )(*args)


def swap(block, axis, groups=None):
    return lax.all_to_all(block, axis, split_axis=0, concat_axis=0, tiled=True, axis_index_groups=groups)


def per_device(table, values, gates, cotangent, filters, skip_gain):
    shape = functools.partial(jax.ShapeDtypeStruct, dtype=jnp.bfloat16)
    spectrum = jax.ShapeDtypeStruct((WIDTH, 2 * WIDTH), jnp.float32)
    packed = shape((BLOCKS, 2, 8 * WIDTH + 128))
    later = lax.shift_right_logical(np.uint32(LATER), lax.axis_index("ctx").astype(jnp.uint32)) & 1
    place = (later.astype(jnp.int32) * SHARDS + shard_at(lax.axis_index("mp"))).reshape(1)
    skip_rows = jnp.broadcast_to(skip_gain[None, :], (8, WIDTH))
    cube = 2 * WIDTH**3

    block = call(
        outgoing_kernel, (packed,), (place, values, gates, cotangent, filters.T),
        2 * cube, scalars=1, fetched=True,
    )
    block = swap(block, "ctx", [ORDER])
    value, gated, own, sent = call(
        spectra_kernel,
        (spectrum, spectrum, shape((BLOCKS, WIDTH)), shape((SHARDS, BLOCKS, WIDTH))),
        (place, block, table["first"], table["middle"], table["last_by_channel"], table["twist"]),
        18 * cube, scalars=1,
    )
    sent = swap(sent, "mp", [MP_ORDER])
    block = call(
        results_kernel, (packed,),
        (place, sent, own, value, gated, table["first_by_channel"], table["middle"], table["last"], table["twist"]),
        18 * cube, scalars=1,
    )
    block = swap(block, "ctx", [ORDER])
    grad_gates, grad_values, grad_filters = call(
        finished_kernel, (shape(values.shape), shape(values.shape), shape((HALF, WIDTH))),
        (place, block, values, gates, cotangent, skip_rows), 2 * cube, scalars=1,
    )
    return (grad_gates, grad_values, grad_filters.T)


def solution(mesh):
    return jax.shard_map(
        functools.partial(per_device, tables()),
        mesh=mesh,
        in_specs=(P("ctx", "mp"), P("ctx", "mp"), P("ctx", "mp"), P("ctx", "mp"), P("mp")),
        out_specs=(P("ctx", "mp"), P("ctx", "mp"), P("ctx", "mp")),
        check_vma=False,
    )
```

```python
import functools
import math

import jax
import jax.numpy as jnp
import numpy as np
from jax import lax
from jax.experimental import pallas as pl
from jax.experimental.pallas import tpu as pltpu
from jax.sharding import PartitionSpec as P

BLOCKS = 32
HALF = 16
MINE = 8
WIDTH = 256
LENGTH = BLOCKS * WIDTH
SHARDS = 16
ORDER = tuple(HALF * x + z for z in (8, 9, 10, 11, 15, 14, 12, 7, 6, 13, 5, 4, 3, 2, 1, 0) for x in (1, 0))
MP_ORDER = tuple(range(SHARDS))[::-1]
LATER = sum(1 << device for device in ORDER[HALF:])
FACTOR = 1.0 / math.sqrt(LENGTH)
VMEM = 32 * 1024 * 1024


def tables():
    quarter = np.arange(BLOCKS) + 0.25
    outer = 2.0 * np.pi * np.outer(quarter, ORDER) / BLOCKS
    eye = np.eye(MINE)
    cos_rows = np.kron(np.cos(outer), eye)
    sin_rows = np.kron(np.sin(outer), eye)
    first = np.concatenate([cos_rows, -sin_rows], 0)
    last = np.concatenate([cos_rows.T, sin_rows.T], 1)
    by_channel = np.arange(BLOCKS * MINE).reshape(BLOCKS, MINE).T.reshape(-1)
    inner = 2.0 * np.pi * (np.outer(np.arange(WIDTH), np.arange(WIDTH)) % WIDTH) / WIDTH
    cos_in, sin_in = (np.cos(inner), np.sin(inner))
    twist = 2.0 * np.pi * np.outer(quarter, np.arange(WIDTH)) / LENGTH
    low = lambda array: array.astype(np.float32).astype(jnp.bfloat16)
    return dict(
        first=low(first),
        first_by_channel=low(first[:, by_channel]),
        middle=low(np.block([[cos_in, -sin_in], [sin_in, cos_in]])),
        last=low(last),
        last_by_channel=low(last[by_channel]),
        twist=np.stack([np.cos(twist), np.sin(twist)]).astype(np.float32),
    )


def dot(left, right, dims=((1,), (0,))):
    return lax.dot_general(
        left.astype(jnp.bfloat16),
        right.astype(jnp.bfloat16),
        (dims, ((), ())),
        preferred_element_type=jnp.float32,
    )


def shard_at(place):
    return SHARDS - 1 - place


def source_of(half, row, place):
    return jnp.where(row == 0, 8 * half + (place & 7), (place - row - 8 * half) & 15)


def order_of(place):
    row = lax.broadcasted_iota(jnp.int32, (WIDTH, 1), 0)
    channel = lax.broadcasted_iota(jnp.int32, (WIDTH, WIDTH), 1)
    wanted = 16 * shard_at(source_of(row >> 7, row & 7, place)) + ((row >> 3) & 15)
    return (channel == wanted).astype(jnp.float32).astype(jnp.bfloat16)


def twisted(real, imag, twist):
    shape = (BLOCKS, MINE, WIDTH)
    cos, sin = (twist[0][:, None, :], twist[1][:, None, :])
    real, imag = (real.reshape(shape), imag.reshape(shape))
    both = [real * cos + imag * sin, imag * cos - real * sin]
    return [part.reshape(WIDTH, WIDTH) for part in both]


def cut(array, step, axis):
    return [lax.slice_in_dim(array, at, at + step, axis=axis) for at in range(0, array.shape[axis], step)]


def forward(signals, first, middle, twist):
    both = [cut(part, WIDTH, 0) for part in cut(dot(first, jnp.concatenate(signals, 1)), WIDTH, 1)]
    both = [jnp.concatenate(twisted(*parts, twist), 1) for parts in both]
    return cut(dot(jnp.concatenate(both, 0), middle), WIDTH, 0)


def inverse(spectra, middle, last, twist):
    both = jnp.concatenate([jnp.concatenate(parts, 1) for parts in spectra], 0)
    both = [cut(part, WIDTH, 1) for part in cut(dot(both, middle), WIDTH, 0)]
    both = [jnp.concatenate(twisted(*parts, twist), 0) for parts in both]
    return cut(dot(last, jnp.concatenate(both, 1)), WIDTH, 1)


def parts_of(spectrum):
    return (spectrum[:, :WIDTH], spectrum[:, WIDTH:])


def pack(upper, lower, extra):
    pieces = []
    for rows in (upper, lower):
        rows = rows.reshape(BLOCKS, MINE, WIDTH)
        pieces += [rows[:, at : at + 2, :] for at in range(0, MINE, 2)]
    spread = [piece[:, None, :] for piece in (extra[:, :128], extra[:, 128:])]
    pieces.append(jnp.concatenate(spread, 1))
    return jnp.concatenate(pieces, 2).astype(jnp.bfloat16)


def rows_of(block, at):
    start = 4 * WIDTH * at
    block = block[:, :, start : start + 4 * WIDTH].astype(jnp.float32)
    rows = jnp.concatenate([block[:, :, k * WIDTH : (k + 1) * WIDTH] for k in range(4)], 1)
    return rows.reshape(BLOCKS * MINE, WIDTH)


def extra_of(block):
    block = block[:, :, 8 * WIDTH :].astype(jnp.float32)
    return jnp.concatenate([block[:, 0], block[:, 1]], 1)


def product_of(cotangent, gates):
    return (cotangent.astype(jnp.float32) * gates.astype(jnp.float32)).astype(jnp.bfloat16)


def packed_rows(order, signal):
    return dot(order, signal, ((1,), (1,)))


def spectra(block, first, middle, last_by_channel, twist):
    value, gated = forward([rows_of(block, 0), rows_of(block, 1)], first, middle, twist)
    (value_r, value_i), (gated_r, gated_i) = (parts_of(value), parts_of(gated))
    lag_spec = (gated_r * value_r + gated_i * value_i, gated_r * value_i - gated_i * value_r)
    (lagged,) = inverse([lag_spec], middle, last_by_channel, twist)
    lagged = (lagged * (1.0 / LENGTH)).reshape(MINE, BLOCKS, WIDTH)
    return (value, gated, lagged.astype(jnp.bfloat16), extra_of(block).astype(jnp.bfloat16))


def results(filters, total, value, gated, first_by_channel, middle, last, twist):
    (filt,) = forward([filters.reshape(MINE * BLOCKS, WIDTH)], first_by_channel, middle, twist)
    (filt_r, filt_i) = parts_of(filt)
    (value_r, value_i), (gated_r, gated_i) = (parts_of(value), parts_of(gated))
    conv_spec = (filt_r * value_r - filt_i * value_i, -filt_r * value_i - filt_i * value_r)
    back_spec = (filt_r * gated_r + filt_i * gated_i, filt_i * gated_r - filt_r * gated_i)
    conv, back = inverse([conv_spec, back_spec], middle, last, twist)
    scale = FACTOR / LENGTH
    return pack(conv * scale, back * scale, total * FACTOR)


def finished(place, block, values, gates, cotangent, skip_rows):
    down = ((0,), (0,))
    order = order_of(place)
    conv = dot(rows_of(block, 0), order, down)
    back = dot(rows_of(block, 1), order, down)
    gated = product_of(cotangent, gates).astype(jnp.float32)
    grad_gates = cotangent.astype(jnp.float32) * (conv + skip_rows[:1] * values.astype(jnp.float32))
    grad_values = back + skip_rows[:1] * gated
    partial = extra_of(block)
    grad_filters = partial[:HALF] + partial[HALF:]
    return tuple(out.astype(jnp.bfloat16) for out in (grad_gates, grad_values, grad_filters))


def outgoing_kernel(place, values, gates, cotangent, filters, out, *scratch):
    held, sems = (scratch[:-1], scratch[-1])
    copies = []
    for at, (source, target) in enumerate(zip((values, gates, cotangent, filters), held)):
        copies.append(pltpu.make_async_copy(source, target, sems.at[at]))
        copies[-1].start()
    order = order_of(place[0] & 15)
    for copy in copies:
        copy.wait()
    value_rows = packed_rows(order, held[0][...])
    gated_rows = packed_rows(order, product_of(held[2][...], held[1][...]))
    filter_rows = jnp.concatenate([held[3][...]] * 2, 0).astype(jnp.float32)
    out[...] = pack(value_rows, gated_rows, filter_rows)


def spectra_kernel(place, *refs):
    half, place = (place[0] >> 4, place[0] & 15)
    value, gated, own, sent = refs[-4:]
    value[...], gated[...], lagged, own_rows = spectra(*(ref[...] for ref in refs[:-4]))
    own[...] = own_rows
    sent[...] = jnp.broadcast_to(own_rows[None], sent.shape)
    for row in range(MINE):
        sent[source_of(half, row, place)] = lagged[row]


def results_kernel(place, arrived, own, *refs):
    half, place = (place[0] >> 4, place[0] & 15)
    held = source_of(half, 0, place) == place
    filters = [jnp.where(held, own[...], arrived[source_of(half, 0, place)])]
    filters += [arrived[source_of(half, row, place)] for row in range(1, MINE)]
    total = jnp.zeros((BLOCKS, WIDTH), jnp.float32)
    for other in range(SHARDS):
        ahead = (other - place) & 15
        near = (ahead >= 1) & (ahead <= 7) | (place == other & 7)
        total += jnp.where(near == (half == 0), arrived[other].astype(jnp.float32), 0.0)
    refs[-1][...] = results(jnp.stack(filters), total, *(ref[...] for ref in refs[:-1]))


def finished_kernel(place, *refs):
    outs = finished(place[0] & 15, *(ref[...] for ref in refs[:-3]))
    for ref, out in zip(refs[-3:], outs):
        ref[...] = out


def call(kernel, outs, args, flops, scalars=0, fetched=False):
    whole = pl.BlockSpec(memory_space=pltpu.VMEM)
    scalar = pl.BlockSpec(memory_space=pltpu.SMEM)
    given = pl.BlockSpec(memory_space=pl.ANY) if fetched else whole
    size = sum(math.prod(out.shape) * out.dtype.itemsize for out in (*outs, *args))
    single = len(outs) == 1
    scratch = []
    if fetched:
        args = (*args[:scalars], *(pltpu.with_memory_space_constraint(arg, pltpu.HBM) for arg in args[scalars:]))
        scratch = [pltpu.VMEM(arg.shape, arg.dtype) for arg in args[scalars:]]
        scratch.append(pltpu.SemaphoreType.DMA((len(scratch),)))
    return pl.pallas_call(
        kernel,
        out_shape=outs[0] if single else outs,
        in_specs=[scalar] * scalars + [given] * (len(args) - scalars),
        out_specs=whole if single else (whole,) * len(outs),
        scratch_shapes=scratch,
        compiler_params=pltpu.CompilerParams(vmem_limit_bytes=VMEM),
        cost_estimate=pl.CostEstimate(flops=flops, bytes_accessed=size, transcendentals=0),
    )(*args)


def swap(block, axis, groups=None):
    return lax.all_to_all(block, axis, split_axis=0, concat_axis=0, tiled=True, axis_index_groups=groups)


def per_device(table, values, gates, cotangent, filters, skip_gain):
    shape = functools.partial(jax.ShapeDtypeStruct, dtype=jnp.bfloat16)
    spectrum = jax.ShapeDtypeStruct((WIDTH, 2 * WIDTH), jnp.float32)
    packed = shape((BLOCKS, 2, 8 * WIDTH + 128))
    later = lax.shift_right_logical(np.uint32(LATER), lax.axis_index("ctx").astype(jnp.uint32)) & 1
    place = (later.astype(jnp.int32) * SHARDS + shard_at(lax.axis_index("mp"))).reshape(1)
    skip_rows = jnp.broadcast_to(skip_gain[None, :], (8, WIDTH))
    cube = 2 * WIDTH**3

    block = call(
        outgoing_kernel, (packed,), (place, values, gates, cotangent, filters.T),
        2 * cube, scalars=1, fetched=True,
    )
    block = swap(block, "ctx", [ORDER])
    value, gated, own, sent = call(
        spectra_kernel,
        (spectrum, spectrum, shape((BLOCKS, WIDTH)), shape((SHARDS, BLOCKS, WIDTH))),
        (place, block, table["first"], table["middle"], table["last_by_channel"], table["twist"]),
        18 * cube, scalars=1,
    )
    sent = swap(sent, "mp", [MP_ORDER])
    block = call(
        results_kernel, (packed,),
        (place, sent, own, value, gated, table["first_by_channel"], table["middle"], table["last"], table["twist"]),
        18 * cube, scalars=1,
    )
    block = swap(block, "ctx", [ORDER])
    grad_gates, grad_values, grad_filters = call(
        finished_kernel, (shape(values.shape), shape(values.shape), shape((HALF, WIDTH))),
        (place, block, values, gates, cotangent, skip_rows), 2 * cube, scalars=1,
    )
    return (grad_gates, grad_values, grad_filters.T)


def solution(mesh):
    return jax.shard_map(
        functools.partial(per_device, tables()),
        mesh=mesh,
        in_specs=(P("ctx", "mp"), P("ctx", "mp"), P("ctx", "mp"), P("ctx", "mp"), P("mp")),
        out_specs=(P("ctx", "mp"), P("ctx", "mp"), P("ctx", "mp")),
        check_vma=False,
    )
```

```python
import functools
import math

import jax
import jax.numpy as jnp
import numpy as np
from jax import lax
from jax.experimental import pallas as pl
from jax.experimental.pallas import tpu as pltpu
from jax.sharding import PartitionSpec as P

BLOCKS = 32
HALF = 16
MINE = 8
WIDTH = 256
LENGTH = BLOCKS * WIDTH
SHARDS = 16
ORDER = tuple(HALF * x + z for z in (8, 9, 10, 11, 15, 14, 12, 7, 6, 13, 5, 4, 3, 2, 1, 0) for x in (1, 0))
MP_ORDER = (14, 10, 6, 2, 12, 8, 4, 0, 15, 11, 7, 3, 13, 9, 5, 1)
LATER = sum(1 << device for device in ORDER[HALF:])
FACTOR = 1.0 / math.sqrt(LENGTH)
VMEM = 32 * 1024 * 1024


def tables():
    quarter = np.arange(BLOCKS) + 0.25
    outer = 2.0 * np.pi * np.outer(quarter, ORDER) / BLOCKS
    eye = np.eye(MINE)
    cos_rows = np.kron(np.cos(outer), eye)
    sin_rows = np.kron(np.sin(outer), eye)
    first = np.concatenate([cos_rows, -sin_rows], 0)
    last = np.concatenate([cos_rows.T, sin_rows.T], 1)
    by_channel = np.arange(BLOCKS * MINE).reshape(BLOCKS, MINE).T.reshape(-1)
    inner = 2.0 * np.pi * (np.outer(np.arange(WIDTH), np.arange(WIDTH)) % WIDTH) / WIDTH
    cos_in, sin_in = (np.cos(inner), np.sin(inner))
    twist = 2.0 * np.pi * np.outer(quarter, np.arange(WIDTH)) / LENGTH
    low = lambda array: array.astype(np.float32).astype(jnp.bfloat16)
    return dict(
        first=low(first),
        first_by_channel=low(first[:, by_channel]),
        middle=low(np.block([[cos_in, -sin_in], [sin_in, cos_in]])),
        last=low(last),
        last_by_channel=low(last[by_channel]),
        twist=np.stack([np.cos(twist), np.sin(twist)]).astype(np.float32),
    )


def dot(left, right, dims=((1,), (0,))):
    return lax.dot_general(
        left.astype(jnp.bfloat16),
        right.astype(jnp.bfloat16),
        (dims, ((), ())),
        preferred_element_type=jnp.float32,
    )


def shard_at(place):
    return 14 - 4 * (place & 3) - 2 * (place >> 2 & 1) + (place >> 3)


def place_of(shard):
    return 8 * (shard & 1) + 4 * (1 - (shard >> 1 & 1)) + 3 - (shard >> 2)


def source_of(half, row, place):
    return jnp.where(row == 0, 8 * half + (place & 7), (place - row - 8 * half) & 15)


def order_of(place):
    row = lax.broadcasted_iota(jnp.int32, (WIDTH, 1), 0)
    channel = lax.broadcasted_iota(jnp.int32, (WIDTH, WIDTH), 1)
    wanted = 16 * shard_at(source_of(row >> 7, row & 7, place)) + ((row >> 3) & 15)
    return (channel == wanted).astype(jnp.float32).astype(jnp.bfloat16)


def twisted(real, imag, twist):
    shape = (BLOCKS, MINE, WIDTH)
    cos, sin = (twist[0][:, None, :], twist[1][:, None, :])
    real, imag = (real.reshape(shape), imag.reshape(shape))
    both = [real * cos + imag * sin, imag * cos - real * sin]
    return [part.reshape(WIDTH, WIDTH) for part in both]


def cut(array, step, axis):
    return [lax.slice_in_dim(array, at, at + step, axis=axis) for at in range(0, array.shape[axis], step)]


def forward(signals, first, middle, twist):
    both = [cut(part, WIDTH, 0) for part in cut(dot(first, jnp.concatenate(signals, 1)), WIDTH, 1)]
    both = [jnp.concatenate(twisted(*parts, twist), 1) for parts in both]
    return cut(dot(jnp.concatenate(both, 0), middle), WIDTH, 0)


def inverse(spectra, middle, last, twist):
    both = jnp.concatenate([jnp.concatenate(parts, 1) for parts in spectra], 0)
    both = [cut(part, WIDTH, 1) for part in cut(dot(both, middle), WIDTH, 0)]
    both = [jnp.concatenate(twisted(*parts, twist), 0) for parts in both]
    return cut(dot(last, jnp.concatenate(both, 1)), WIDTH, 1)


def parts_of(spectrum):
    return (spectrum[:, :WIDTH], spectrum[:, WIDTH:])


def pack(upper, lower, extra):
    pieces = []
    for rows in (upper, lower):
        rows = rows.reshape(BLOCKS, MINE, WIDTH)
        pieces += [rows[:, at : at + 2, :] for at in range(0, MINE, 2)]
    spread = [piece[:, None, :] for piece in (extra[:, :128], extra[:, 128:])]
    pieces.append(jnp.concatenate(spread, 1))
    return jnp.concatenate(pieces, 2).astype(jnp.bfloat16)


def rows_of(block, at):
    start = 4 * WIDTH * at
    block = block[:, :, start : start + 4 * WIDTH].astype(jnp.float32)
    rows = jnp.concatenate([block[:, :, k * WIDTH : (k + 1) * WIDTH] for k in range(4)], 1)
    return rows.reshape(BLOCKS * MINE, WIDTH)


def extra_of(block):
    block = block[:, :, 8 * WIDTH :].astype(jnp.float32)
    return jnp.concatenate([block[:, 0], block[:, 1]], 1)


def product_of(cotangent, gates):
    return (cotangent.astype(jnp.float32) * gates.astype(jnp.float32)).astype(jnp.bfloat16)


def packed_rows(order, signal):
    return dot(order, signal, ((1,), (1,)))


def spectra(block, first, middle, last_by_channel, twist):
    value, gated = forward([rows_of(block, 0), rows_of(block, 1)], first, middle, twist)
    (value_r, value_i), (gated_r, gated_i) = (parts_of(value), parts_of(gated))
    lag_spec = (gated_r * value_r + gated_i * value_i, gated_r * value_i - gated_i * value_r)
    (lagged,) = inverse([lag_spec], middle, last_by_channel, twist)
    lagged = (lagged * (1.0 / LENGTH)).reshape(MINE, BLOCKS, WIDTH)
    return (value, gated, lagged.astype(jnp.bfloat16), extra_of(block).astype(jnp.bfloat16))


def results(filters, total, value, gated, first_by_channel, middle, last, twist):
    (filt,) = forward([filters.reshape(MINE * BLOCKS, WIDTH)], first_by_channel, middle, twist)
    (filt_r, filt_i) = parts_of(filt)
    (value_r, value_i), (gated_r, gated_i) = (parts_of(value), parts_of(gated))
    conv_spec = (filt_r * value_r - filt_i * value_i, -filt_r * value_i - filt_i * value_r)
    back_spec = (filt_r * gated_r + filt_i * gated_i, filt_i * gated_r - filt_r * gated_i)
    conv, back = inverse([conv_spec, back_spec], middle, last, twist)
    scale = FACTOR / LENGTH
    return pack(conv * scale, back * scale, total * FACTOR)


def finished(place, block, values, gates, cotangent, skip_rows):
    down = ((0,), (0,))
    order = order_of(place)
    conv = dot(rows_of(block, 0), order, down)
    back = dot(rows_of(block, 1), order, down)
    gated = product_of(cotangent, gates).astype(jnp.float32)
    grad_gates = cotangent.astype(jnp.float32) * (conv + skip_rows[:1] * values.astype(jnp.float32))
    grad_values = back + skip_rows[:1] * gated
    partial = extra_of(block)
    grad_filters = partial[:HALF] + partial[HALF:]
    return tuple(out.astype(jnp.bfloat16) for out in (grad_gates, grad_values, grad_filters))


def outgoing_kernel(place, values, gates, cotangent, filters, out, *scratch):
    held, sems = (scratch[:-1], scratch[-1])
    copies = []
    for at, (source, target) in enumerate(zip((values, gates, cotangent, filters), held)):
        copies.append(pltpu.make_async_copy(source, target, sems.at[at]))
        copies[-1].start()
    order = order_of(place[0] & 15)
    for copy in copies:
        copy.wait()
    value_rows = packed_rows(order, held[0][...])
    gated_rows = packed_rows(order, product_of(held[2][...], held[1][...]))
    filter_rows = jnp.concatenate([held[3][...]] * 2, 0).astype(jnp.float32)
    out[...] = pack(value_rows, gated_rows, filter_rows)


def spectra_kernel(place, *refs):
    half, place = (place[0] >> 4, place[0] & 15)
    value, gated, own, sent = refs[-4:]
    value[...], gated[...], lagged, own_rows = spectra(*(ref[...] for ref in refs[:-4]))
    own[...] = own_rows
    sent[...] = jnp.broadcast_to(own_rows[None], sent.shape)
    for row in range(MINE):
        sent[source_of(half, row, place)] = lagged[row]


def results_kernel(place, arrived, own, *refs):
    half, place = (place[0] >> 4, place[0] & 15)
    held = source_of(half, 0, place) == place
    filters = [jnp.where(held, own[...], arrived[source_of(half, 0, place)])]
    filters += [arrived[source_of(half, row, place)] for row in range(1, MINE)]
    total = jnp.zeros((BLOCKS, WIDTH), jnp.float32)
    for other in range(SHARDS):
        ahead = (other - place) & 15
        near = (ahead >= 1) & (ahead <= 7) | (place == other & 7)
        total += jnp.where(near == (half == 0), arrived[other].astype(jnp.float32), 0.0)
    refs[-1][...] = results(jnp.stack(filters), total, *(ref[...] for ref in refs[:-1]))


def finished_kernel(place, *refs):
    outs = finished(place[0] & 15, *(ref[...] for ref in refs[:-3]))
    for ref, out in zip(refs[-3:], outs):
        ref[...] = out


def call(kernel, outs, args, flops, scalars=0, fetched=False):
    whole = pl.BlockSpec(memory_space=pltpu.VMEM)
    scalar = pl.BlockSpec(memory_space=pltpu.SMEM)
    given = pl.BlockSpec(memory_space=pl.ANY) if fetched else whole
    size = sum(math.prod(out.shape) * out.dtype.itemsize for out in (*outs, *args))
    single = len(outs) == 1
    scratch = []
    if fetched:
        args = (*args[:scalars], *(pltpu.with_memory_space_constraint(arg, pltpu.HBM) for arg in args[scalars:]))
        scratch = [pltpu.VMEM(arg.shape, arg.dtype) for arg in args[scalars:]]
        scratch.append(pltpu.SemaphoreType.DMA((len(scratch),)))
    return pl.pallas_call(
        kernel,
        out_shape=outs[0] if single else outs,
        in_specs=[scalar] * scalars + [given] * (len(args) - scalars),
        out_specs=whole if single else (whole,) * len(outs),
        scratch_shapes=scratch,
        compiler_params=pltpu.CompilerParams(vmem_limit_bytes=VMEM),
        cost_estimate=pl.CostEstimate(flops=flops, bytes_accessed=size, transcendentals=0),
    )(*args)


def swap(block, axis, groups=None):
    return lax.all_to_all(block, axis, split_axis=0, concat_axis=0, tiled=True, axis_index_groups=groups)


def per_device(table, values, gates, cotangent, filters, skip_gain):
    shape = functools.partial(jax.ShapeDtypeStruct, dtype=jnp.bfloat16)
    spectrum = jax.ShapeDtypeStruct((WIDTH, 2 * WIDTH), jnp.float32)
    packed = shape((BLOCKS, 2, 8 * WIDTH + 128))
    later = lax.shift_right_logical(np.uint32(LATER), lax.axis_index("ctx").astype(jnp.uint32)) & 1
    place = (later.astype(jnp.int32) * SHARDS + place_of(lax.axis_index("mp"))).reshape(1)
    skip_rows = jnp.broadcast_to(skip_gain[None, :], (8, WIDTH))
    cube = 2 * WIDTH**3

    block = call(
        outgoing_kernel, (packed,), (place, values, gates, cotangent, filters.T),
        2 * cube, scalars=1, fetched=True,
    )
    block = swap(block, "ctx", [ORDER])
    value, gated, own, sent = call(
        spectra_kernel,
        (spectrum, spectrum, shape((BLOCKS, WIDTH)), shape((SHARDS, BLOCKS, WIDTH))),
        (place, block, table["first"], table["middle"], table["last_by_channel"], table["twist"]),
        18 * cube, scalars=1,
    )
    sent = swap(sent, "mp", [MP_ORDER])
    block = call(
        results_kernel, (packed,),
        (place, sent, own, value, gated, table["first_by_channel"], table["middle"], table["last"], table["twist"]),
        18 * cube, scalars=1,
    )
    block = swap(block, "ctx", [ORDER])
    grad_gates, grad_values, grad_filters = call(
        finished_kernel, (shape(values.shape), shape(values.shape), shape((HALF, WIDTH))),
        (place, block, values, gates, cotangent, skip_rows), 2 * cube, scalars=1,
    )
    return (grad_gates, grad_values, grad_filters.T)


def solution(mesh):
    return jax.shard_map(
        functools.partial(per_device, tables()),
        mesh=mesh,
        in_specs=(P("ctx", "mp"), P("ctx", "mp"), P("ctx", "mp"), P("ctx", "mp"), P("mp")),
        out_specs=(P("ctx", "mp"), P("ctx", "mp"), P("ctx", "mp")),
        check_vma=False,
    )
```
